512 devices in a mesh: dp: 64 (over x, z), mp: 8 (over y, core).
Axes of the slice: x: 4, y: 4, z: 16, core: 2. Of those that a mesh axis runs over, the one named last changes fastest.
Arguments:
- queries: bfloat16 [32768, 2048], P('dp', 'mp'), may hold values from -6 to 6
- states: bfloat16 [256, 128, 448], P('dp', 'mp'), may hold values from -6 to 6
- gain: float32 [448], replicated, may hold values from 0.1 to 1.9
- w_kv: bfloat16 [2, 448, 2048], P(None, None, 'mp'), may hold values from -0.25 to 0.25
- neighbour_ids: int32 [512, 2], P('dp'), may hold values from 0 to 255, as said below
- block_place: int32 [256], replicated, may hold values from 0 to 255, as said below
- grad_out: bfloat16 [32768, 2048], P('dp', 'mp'), may hold values from -6 to 6
Outputs:
- attended: bfloat16 [32768, 2048], P('dp', 'mp')
- grad_queries: bfloat16 [32768, 2048], P('dp', 'mp')
- grad_kv: bfloat16 [2, 448, 2048], P(None, None, 'mp')
- grad_gain: float32 [448], replicated
The draws below stay inside these ranges and needn't reach their ends.
Inputs may be any that keep to these rules, and one draw needn't show every extreme that they name: `neighbour_ids`: of the 16 ids named by the blocks of one dp index, at most 2 lie on any one owner (owner = block_place[id] // 4); one owner, the same for every dp index, holds exactly 2 of them for every dp index. `block_place`: A permutation of the ids.
All inputs are finite; a program needn't handle non-finite values.
Results may differ from the reference program's by a relative error of at most 0.015.
Values may be sent and summed in bfloat16 or wider, within the bound.
A program may use at most 64 MiB of HBM per device.

```python
import jax
import jax.numpy as jnp
from jax import lax

HEADS = 16
HD = 128
DE = 448
BLOCK = 64
NEIGH = 2
NTOK = 128
CAP = 2
TOK_DEV = 512
OWN_DEV = 4
D = 2048
TOKENS = 32768
POOL = 256
N_DP = 64
N_MP = 8


def layout(key):
    return jax.random.permutation(key, POOL).astype(jnp.int32)


def draw_block_place(key, part):
    return layout(key)


def draw_neighbour_ids(key, part):
    place = layout(key)
    key = jax.random.fold_in(key, 7)
    devices = TOKENS // TOK_DEV
    per_dev = TOK_DEV // BLOCK * NEIGH
    groups = per_dev // CAP
    hot = jax.random.randint(jax.random.fold_in(key, 1), (), 0, devices).astype(jnp.int32)

    def one(index):
        sub = jax.random.fold_in(key, index + 2)
        first, second, third = jax.random.split(sub, 3)
        others = jax.random.permutation(first, devices - 1)[:groups - 1].astype(jnp.int32)
        others = others + (others >= hot).astype(jnp.int32)
        owners = jnp.repeat(jnp.concatenate([hot[None], others]), CAP)
        owners = owners[jax.random.permutation(second, per_dev)]
        slots = jax.random.randint(third, (per_dev,), 0, OWN_DEV).astype(jnp.int32)
        return owners * OWN_DEV + slots
    positions = jax.vmap(one)(jnp.arange(devices))
    inverse = jnp.argsort(place, stable=True).astype(jnp.int32)
    ids = inverse[positions.reshape(-1)]
    return ids.reshape(TOKENS // BLOCK, NEIGH).astype(jnp.int32)


def level_of(stream_key, extent, shards, low, top_value):
    def one(axis_at, shards_of):
        heights = jax.random.uniform(jax.random.fold_in(jax.random.fold_in(stream_key, 6), axis_at), (shards_of,), jnp.float32, low / len(shards), top_value / len(shards))
        return jnp.repeat(jnp.exp(heights), extent[axis_at] // shards_of).reshape((-1,) + (1,) * (len(extent) - axis_at - 1))

    factor_of = one(*shards[0])
    for cut in shards[1:]:
        factor_of = factor_of * one(*cut)
    return factor_of


def scatter_about(stream_key, dims, spread, most, pieces=(), dtype=jnp.bfloat16):
    loudness = level_of(stream_key, dims, pieces, -0.22, 0.18) if pieces else 1.0
    values = jax.random.normal(stream_key, dims, jnp.float32) * spread * loudness
    return jnp.minimum(jnp.maximum(values, -most), most).astype(dtype)


def setup_inputs(seed: int = 0) -> dict:
    seeds = jax.random.split(jax.random.key(seed), 8)
    queries = scatter_about(seeds[0], (TOKENS, D), 1.0, 6.0, ((0, 64), (1, 8)))
    states = scatter_about(seeds[1], (POOL, NTOK, DE), 1.0, 6.0, ((0, 64), (1, 8)))
    gain = jnp.clip(1.0 + 0.18 * jax.random.normal(seeds[2], (DE,), jnp.float32), 0.1, 1.9)
    w_kv = scatter_about(seeds[3], (2, DE, D), DE ** -0.5, 0.25, ((2, 8),))
    neighbour_ids = draw_neighbour_ids(jax.random.fold_in(seeds[7], 71), 0)
    block_place = draw_block_place(jax.random.fold_in(seeds[7], 71), 0)
    grad_out = scatter_about(seeds[6], (TOKENS, D), 1.0, 6.0, ((0, 64), (1, 8)))
    return {"queries": queries, "states": states, "gain": gain, "w_kv": w_kv, "neighbour_ids": neighbour_ids, "block_place": block_place, "grad_out": grad_out}


def reference(queries, states, gain, w_kv, neighbour_ids, block_place, grad_out):
    statef = states.astype(jnp.float32)
    normed = statef * lax.rsqrt(lax.optimization_barrier(jnp.mean(statef * statef, -1, keepdims=True)) + 1e-06)
    encoded = (normed * gain).astype(jnp.bfloat16)
    placed = block_place[neighbour_ids].astype(jnp.int32)
    units = TOK_DEV // BLOCK
    scale = HD ** (-0.5)
    group_cols = HEADS * HD // N_MP
    query_g = queries.reshape(N_DP, units, BLOCK, HEADS, HD)
    grad_g = grad_out.reshape(N_DP, units, BLOCK, HEADS, HD)
    place_g = placed.reshape(N_DP, units * NEIGH)
    wk_groups = w_kv[0].reshape(DE, N_MP, group_cols).astype(jnp.float32)
    wv_groups = w_kv[1].reshape(DE, N_MP, group_cols).astype(jnp.float32)

    def group(carry, item):
        weight_acc, state_acc = carry
        query_c, grad_c, rows = item
        nbr = encoded[rows].reshape(units * NEIGH * NTOK, DE)
        keys = jnp.dot(nbr, w_kv[0], preferred_element_type=jnp.float32).astype(jnp.bfloat16)
        values = jnp.dot(nbr, w_kv[1], preferred_element_type=jnp.float32).astype(jnp.bfloat16)
        key_c = keys.reshape(units, NEIGH * NTOK, HEADS, HD).astype(jnp.float32)
        value_c = values.reshape(units, NEIGH * NTOK, HEADS, HD).astype(jnp.float32)
        qf = query_c.astype(jnp.float32)
        gf = grad_c.astype(jnp.float32)
        scores = jnp.einsum('uqhd,ukhd->uhqk', qf, key_c) * scale
        probs = jax.nn.softmax(scores, -1)
        probs_b = probs.astype(jnp.bfloat16).astype(jnp.float32)
        attended = jnp.einsum('uhqk,ukhd->uqhd', probs_b, value_c).astype(jnp.bfloat16)
        d_probs = jnp.einsum('uqhd,ukhd->uhqk', gf, value_c)
        delta = lax.optimization_barrier(jnp.sum(d_probs * probs, -1, keepdims=True))
        d_scores = (probs * (d_probs - delta) * scale).astype(jnp.bfloat16).astype(jnp.float32)
        d_query = jnp.einsum('uhqk,ukhd->uqhd', d_scores, key_c).astype(jnp.bfloat16)
        d_value = jnp.einsum('uhqk,uqhd->ukhd', probs_b, gf).astype(jnp.bfloat16).reshape(-1, HEADS * HD)
        d_key = jnp.einsum('uhqk,uqhd->ukhd', d_scores, qf).astype(jnp.bfloat16).reshape(-1, HEADS * HD)
        weight_acc = weight_acc + jnp.stack([jnp.dot(nbr.T, d_key, preferred_element_type=jnp.float32), jnp.dot(nbr.T, d_value, preferred_element_type=jnp.float32)])
        dk_groups = d_key.reshape(-1, N_MP, group_cols).astype(jnp.float32)
        dv_groups = d_value.reshape(-1, N_MP, group_cols).astype(jnp.float32)
        terms = jnp.einsum('rgc,egc->gre', dk_groups, wk_groups) + jnp.einsum('rgc,egc->gre', dv_groups, wv_groups)
        terms = lax.optimization_barrier(terms.astype(jnp.bfloat16)).astype(jnp.float32)
        d_neigh = lax.optimization_barrier(jnp.sum(terms, 0)).astype(jnp.bfloat16)
        state_acc = state_acc.at[rows].add(d_neigh.reshape(units * NEIGH, NTOK, DE).astype(jnp.float32))
        return ((weight_acc, state_acc), (attended, d_query))
    start = (jnp.zeros((2, DE, HEADS * HD), jnp.float32), jnp.zeros((POOL, NTOK, DE), jnp.float32))
    (weight_acc, d_encoded), (attended, d_query) = lax.scan(group, start, (query_g, grad_g, place_g))
    grad_gain = lax.optimization_barrier(jnp.sum(d_encoded * normed, axis=(0, 1)))
    return (attended.reshape(TOKENS, HEADS * HD), d_query.reshape(TOKENS, HEADS * HD), weight_acc.astype(jnp.bfloat16), grad_gain)
```

```python
import functools

import jax
import jax.numpy as jnp
from jax import lax
from jax.experimental import pallas as pl
from jax.experimental.pallas import tpu as pltpu
from jax.sharding import PartitionSpec as P

HD = 128
BLOCK = 64
NEIGH = 2
NX, NY, NZ = 4, 4, 16
OWN = 4
UNITS = 8
REQ = 16
SLICE = 16
DE = 448
NMP = 8
PIECE = 32
NPIECE = DE // PIECE
QUARTERS = 4
QSLOTS = REQ // QUARTERS
F32 = jnp.float32
BF16 = jnp.bfloat16
MESH = pl.DeviceIdType.MESH


def dot(a, b, ca, cb):
    return lax.dot_general(a, b, (((ca,), (cb,)), ((), ())), preferred_element_type=F32)


def remote(src, dst, send, recv, to):
    return pltpu.make_async_remote_copy(
        src_ref=src, dst_ref=dst, send_sem=send, recv_sem=recv, device_id=to, device_id_type=MESH
    )


def kernel(
    states_hbm, gain_hbm, ids_hbm, place_hbm, w_hbm, q_hbm, g_hbm,
    out_ref, dq_ref, gkv_ref, ggain_ref,
    states_ref, gain_ref, ids_ref, place_ref, w_ref, q_ref, g_ref, load_sem,
    zbuf, idbuf, ids_s, out_x, from_x, nb,
    grad, xs, xr, acc, zs, rbuf, full, gm, gx, gz,
    id_send, id_recv, id_local, zr_send, zr_recv, zl_send, zl_recv,
    x_send, x_recv, y_send, y_recv, s_send, s_recv,
    rx_send, rx_recv, rz_send, rz_recv, gz_send, gz_recv, gx_send, gx_recv,
    m_send, m_recv, h_send, h_recv, v_send, v_recv,
):
    dp = lax.axis_index("dp")
    mp = lax.axis_index("mp")
    x, z, y, c = dp // NZ, dp % NZ, mp // 2, mp % 2
    to_z = lambda k: (x * NZ + (z + k + NZ) % NZ, mp)
    to_x = lambda k: ((x + k) % NX * NZ + z, mp)
    to_y = lambda k: (dp, (y + k) % NY * 2 + c)
    sib = (dp, y * 2 + 1 - c)
    sent = []

    def start(cp):
        cp.start()
        sent.append(cp)
        return cp

    loads = [
        pltpu.make_async_copy(src, dst, load_sem.at[i])
        for i, (src, dst) in enumerate(
            (
                (states_hbm, states_ref), (gain_hbm, gain_ref), (ids_hbm, ids_ref),
                (place_hbm, place_ref), (w_hbm, w_ref), (q_hbm, q_ref), (g_hbm, g_ref),
            )
        )
    ]
    for cp in loads:
        cp.start()

    barrier = pltpu.get_barrier_semaphore()
    near = [to_z(1), to_z(-1), to_z(2), to_z(-2), to_x(1), to_x(2), to_x(3), to_y(1), to_y(2), to_y(3), sib]
    for peer in near:
        pl.semaphore_signal(barrier, inc=1, device_id=peer, device_id_type=MESH)

    for cp in loads[:4]:
        cp.wait()
    own = states_ref[...].astype(F32)
    normed = own * lax.rsqrt(jnp.mean(own * own, -1, keepdims=True) + 1e-6)
    zbuf[pl.ds(z * OWN, OWN)] = (normed * gain_ref[...]).astype(BF16)
    lane = lax.broadcasted_iota(jnp.int32, (8, 128), 1)
    vec = jnp.zeros((8, 128), jnp.int32)
    for r in range(REQ):
        vec = jnp.where(lane == r, place_ref[ids_ref[r % NEIGH, r // NEIGH]], vec)
    idbuf[x] = vec

    pl.semaphore_wait(barrier, len(near))

    def z_copy(d, half, right):
        st = 1 if d == 1 else 2
        at = ((z - d + st + NZ) % NZ if right else (z + d - st) % NZ) * OWN + half * 2
        ref = zbuf.at[pl.ds(at, 2)]
        if right:
            return remote(ref, ref, zr_send.at[d - 1, half], zr_recv.at[d - 1, half], to_z(st))
        return remote(ref, ref, zl_send.at[d - 1, half], zl_recv.at[d - 1, half], to_z(-st))

    chains = [(True, 0), (False, 1), (True, 1), (False, 0)]
    reach = {(True, 0): 8, (True, 1): 7, (False, 0): 7, (False, 1): 8}
    live = {}
    for d in (2, 1):
        for right, half in chains:
            live[right, half, d] = start(z_copy(d, half, right))
    id_copies = [
        start(remote(idbuf.at[x], idbuf.at[x], id_send.at[k - 1], id_recv.at[k - 1], to_x(k)))
        for k in (2, 1, 3)
    ]
    for d in range(1, 9):
        for right, half in chains:
            n = reach[right, half]
            if d > n:
                continue
            live[right, half, d].wait_recv()
            if d + 2 <= n:
                live[right, half, d + 2] = start(z_copy(d + 2, half, right))
        if d == 2:
            for cp in id_copies:
                cp.wait_recv()
            local = pltpu.make_async_copy(idbuf, ids_s, id_local)
            local.start()
            local.wait()

    def wanted(who, r):
        p = ids_s[who, 0, r]
        return lax.rem(p, NZ * OWN), lax.div(p, NZ * OWN)

    x_copies = {}
    for j in range(QUARTERS):
        for k in (2, 1, 3):
            for r in range(j * QSLOTS, (j + 1) * QSLOTS):
                out_x[k - 1, r] = zbuf[wanted((x + k) % NX, r)[0]]
            slots = pl.ds(j * QSLOTS, QSLOTS)
            x_copies[k, j] = start(
                remote(
                    out_x.at[k - 1, slots], from_x.at[k - 1, slots],
                    x_send.at[k - 1, j], x_recv.at[k - 1, j], to_x(k),
                )
            )

    y_copies, s_copies = {}, {}

    def finish(j):
        for k in (1, 3, 2):
            x_copies[k, j].wait_recv()
        for r in range(j * QSLOTS, (j + 1) * QSLOTS):
            at, col = wanted(x, r)
            block = zbuf[at]
            for k in (1, 2, 3):
                block = jnp.where(col == (x + NX - k) % NX, from_x[k - 1, r], block)
            nb[mp, r] = block
        ref = nb.at[mp, pl.ds(j * QSLOTS, QSLOTS)]
        for k in (2, 1, 3):
            y_copies[k, j] = start(remote(ref, ref, y_send.at[k - 1, j], y_recv.at[k - 1, j], to_y(k)))
        s_copies[0, j] = start(remote(ref, ref, s_send.at[0, j], s_recv.at[0, j], sib))

    def relay(j):
        for k in (1, 3, 2):
            y_copies[k, j].wait_recv()
            ref = nb.at[(y + NY - k) % NY * 2 + c, pl.ds(j * QSLOTS, QSLOTS)]
            s_copies[k, j] = start(remote(ref, ref, s_send.at[k, j], s_recv.at[k, j], sib))

    scale = HD ** (-0.5)

    def attend(j):
        for k in range(4):
            s_copies[k, j].wait_recv()
        units = range(2 * j, 2 * j + 2)
        encs = [nb[:, NEIGH * u:NEIGH * (u + 1)].reshape(NMP * NEIGH * SLICE, DE) for u in units]
        keys = [dot(e, w_ref[0], 1, 0).astype(BF16) for e in encs]
        values = [dot(e, w_ref[1], 1, 0).astype(BF16) for e in encs]
        cells = []
        for i, u in enumerate(units):
            for h in range(2):
                rows, cols = slice(u * BLOCK, (u + 1) * BLOCK), slice(h * HD, (h + 1) * HD)
                cells.append((rows, cols, q_ref[rows, cols], g_ref[rows, cols], keys[i][:, cols], values[i][:, cols]))
        ss = [dot(q, k, 1, 1) * scale for _, _, q, g, k, v in cells]
        dps = [dot(g, v, 1, 1) for _, _, q, g, k, v in cells]
        es = [jnp.exp(s - jnp.max(s, -1, keepdims=True)) for s in ss]
        ps = [e / jnp.sum(e, -1, keepdims=True) for e in es]
        pbs = [p.astype(BF16) for p in ps]
        dss = [
            (p * (dp_ - jnp.sum(dp_ * p, -1, keepdims=True)) * scale).astype(BF16)
            for p, dp_ in zip(ps, dps)
        ]
        dks, dvs = [], []
        for (rows, cols, q, g, k, v), pb, ds in zip(cells, pbs, dss):
            out_ref[rows, cols] = dot(pb, v, 1, 0).astype(BF16)
            dq_ref[rows, cols] = dot(ds, k, 1, 0).astype(BF16)
            dks.append(dot(ds, q, 0, 0).astype(BF16))
            dvs.append(dot(pb, g, 0, 0).astype(BF16))
        enc = jnp.concatenate(encs, axis=0)
        dk = jnp.concatenate([jnp.concatenate(dks[0:2], axis=1), jnp.concatenate(dks[2:4], axis=1)], axis=0)
        dv = jnp.concatenate([jnp.concatenate(dvs[0:2], axis=1), jnp.concatenate(dvs[2:4], axis=1)], axis=0)
        for side, d in enumerate((dk, dv)):
            total = dot(enc, d, 0, 0)
            for h in range(2):
                part = total[:, h * HD:(h + 1) * HD]
                if j == 0:
                    grad[2 * side + h] = part
                else:
                    grad[2 * side + h] += part

    for step in range(QUARTERS + 2):
        if step < QUARTERS:
            finish(step)
        if 0 <= step - 1 < QUARTERS:
            relay(step - 1)
        if step == 2:
            for cp in loads[4:]:
                cp.wait()
        if 0 <= step - 2 < QUARTERS:
            attend(step - 2)

    HALF = DE // 2
    rx = {}
    for half in range(2):
        span = slice(half * HALF, (half + 1) * HALF)
        at = pl.ds(half * HALF, HALF)
        for k in (2, 1, 3):
            xs[k - 1, span] = grad[(x + k) % NX, span].astype(BF16)
            rx[k, half] = start(
                remote(xs.at[k - 1, at], xr.at[k - 1, at], rx_send.at[k - 1, half], rx_recv.at[k - 1, half], to_x(k))
            )

    prod = jnp.zeros((DE, HD), F32)
    for j in range(4):
        prod = prod + w_ref[j // 2, :, (j % 2) * HD:(j % 2 + 1) * HD].astype(F32) * grad[j]
    part = lax.dot_general(
        jnp.ones((8, HD), F32), prod, (((1,), (1,)), ((), ())),
        precision=lax.Precision.HIGHEST, preferred_element_type=F32,
    )[0:1] / gain_ref[...]
    tail = jnp.concatenate([part[:, 384:448], jnp.zeros((1, 64), F32)], axis=1)
    gm[mp] = jnp.concatenate(
        [part[:, 0:128], part[:, 128:256], part[:, 256:384], tail, jnp.zeros((4, 128), F32)], axis=0
    )
    m_copies = [
        start(remote(gm.at[mp], gm.at[mp], m_send.at[k - 1], m_recv.at[k - 1], (dp, (mp + k) % NMP)))
        for k in range(1, NMP)
    ]

    def rows_of(t):
        return pl.ds(pl.multiple_of((t // 2 + NPIECE // 2 * (t % 2)) * PIECE, PIECE), PIECE)

    def z_out(t):
        return remote(zs.at[rows_of(t)], rbuf.at[z], rz_send.at[t], rz_recv.at[z], (x * NZ + t, mp))

    def sum_x(half):
        for k in (1, 3, 2):
            rx[k, half].wait_recv()
        span = slice(half * HALF, (half + 1) * HALF)
        total = grad[x, span]
        for k in (1, 2, 3):
            total = total + xr[k - 1, span].astype(F32)
        acc[span] = total
        zs[span] = total.astype(BF16)
        for t in range(half, NPIECE, 2):
            pl.when(z != t)(z_out(t).start)

    sum_x(0)
    for cp in m_copies:
        cp.wait_recv()
    gx[x] = functools.reduce(lambda s, m: s + gm[m], range(1, NMP), gm[0])
    h_copies = [
        start(remote(gx.at[x], gx.at[x], h_send.at[k - 1], h_recv.at[k - 1], to_x(k))) for k in (2, 1, 3)
    ]
    sum_x(1)
    for cp in h_copies:
        cp.wait_recv()
    gz[z] = functools.reduce(lambda s, m: s + gx[m], range(1, NX), gx[0])
    v_copies = [
        start(remote(gz.at[z], gz.at[z], v_send.at[k - 1], v_recv.at[k - 1], to_z(k)))
        for k in range(1, NZ)
    ]

    def z_back(k):
        ref = full.at[x, rows_of(z)]
        return remote(ref, ref, gz_send.at[k - 1], gz_recv.at[z], to_z(k))

    @pl.when(z < NPIECE)
    def _():
        rbuf[z] = jnp.zeros((PIECE, HD), BF16)
        for s in range(NZ):
            arrival = remote(zs.at[rows_of(0)], rbuf.at[s], rz_send.at[s], rz_recv.at[s], to_z(1))
            pl.when(z != s)(arrival.wait_recv)
        total = acc[rows_of(z)]
        for s in range(NZ):
            total = total + rbuf[s].astype(F32)
        full[x, rows_of(z)] = total.astype(BF16)
        for k in range(1, NZ):
            z_back(k).start()

    back = {}
    for half in range(2):
        for t in range(half, NPIECE, 2):
            ref = full.at[x, rows_of(t)]
            pl.when(z != t)(remote(ref, ref, gz_send.at[0], gz_recv.at[t], to_z(1)).wait_recv)
        ref = full.at[x, pl.ds(half * HALF, HALF)]
        for k in (2, 1, 3):
            back[k, half] = start(remote(ref, ref, gx_send.at[k - 1, half], gx_recv.at[k - 1, half], to_x(k)))

    for cp in v_copies:
        cp.wait_recv()
    g = functools.reduce(lambda s, m: s + gz[m], range(1, NZ), gz[0])
    ggain_ref[...] = jnp.concatenate([g[0:1], g[1:2], g[2:3], g[3:4, 0:64]], axis=1)

    for cp in back.values():
        cp.wait_recv()
    for j in range(4):
        gkv_ref[j // 2, :, (j % 2) * HD:(j % 2 + 1) * HD] = full[j]

    for t in range(NPIECE):
        pl.when(z != t)(z_out(t).wait_send)

    @pl.when(z < NPIECE)
    def _():
        for k in range(1, NZ):
            z_back(k).wait_send()

    for cp in sent:
        cp.wait_send()


def body(queries, states, gain, w_kv, neighbour_ids, block_place, grad_out):
    dma = pltpu.SemaphoreType.DMA
    vmem = pltpu.VMEM
    block = (SLICE, DE)
    tok, cols = queries.shape
    any_spec = pl.BlockSpec(memory_space=pl.ANY)
    out_spec = pl.BlockSpec(memory_space=pltpu.VMEM)
    attended, d_query, grad_kv, grad_gain = pl.pallas_call(
        kernel,
        out_shape=(
            jax.ShapeDtypeStruct((tok, cols), BF16),
            jax.ShapeDtypeStruct((tok, cols), BF16),
            jax.ShapeDtypeStruct((2, DE, cols), BF16),
            jax.ShapeDtypeStruct((1, DE), F32),
        ),
        in_specs=[any_spec] * 7,
        out_specs=(out_spec,) * 4,
        scratch_shapes=[
            vmem(states.shape, BF16),
            vmem((1, DE), F32),
            pltpu.SMEM(neighbour_ids.shape[::-1], jnp.int32),
            pltpu.SMEM(block_place.shape, jnp.int32),
            vmem(w_kv.shape, BF16),
            vmem((tok, cols), BF16),
            vmem((tok, cols), BF16),
            dma((7,)),
            vmem((NZ * OWN,) + block, BF16),
            vmem((NX, 8, 128), jnp.int32),
            pltpu.SMEM((NX, 8, 128), jnp.int32),
            vmem((3, REQ) + block, BF16),
            vmem((3, REQ) + block, BF16),
            vmem((NMP, REQ) + block, BF16),
            vmem((4, DE, HD), F32),
            vmem((3, DE, HD), BF16),
            vmem((3, DE, HD), BF16),
            vmem((DE, HD), F32),
            vmem((DE, HD), BF16),
            vmem((NZ, PIECE, HD), BF16),
            vmem((NX, DE, HD), BF16),
            vmem((NMP, 8, 128), F32),
            vmem((NX, 8, 128), F32),
            vmem((NZ, 8, 128), F32),
            dma((3,)), dma((3,)), dma,
            dma((8, 2)), dma((8, 2)), dma((8, 2)), dma((8, 2)),
            dma((3, QUARTERS)), dma((3, QUARTERS)),
            dma((3, QUARTERS)), dma((3, QUARTERS)),
            dma((4, QUARTERS)), dma((4, QUARTERS)),
            dma((3, 2)), dma((3, 2)), dma((NZ,)), dma((NZ,)), dma((NZ,)), dma((NZ,)),
            dma((3, 2)), dma((3, 2)),
            dma((NMP,)), dma((NMP,)), dma((3,)), dma((3,)), dma((NZ,)), dma((NZ,)),
        ],
        compiler_params=pltpu.CompilerParams(
            collective_id=0, has_side_effects=True, vmem_limit_bytes=40 * 1024 * 1024
        ),
        name="retro_step",
    )(states, gain.reshape(1, DE), neighbour_ids.T, block_place, w_kv, queries, grad_out)
    return attended, d_query, grad_kv, grad_gain.reshape(DE)


def solution(mesh):
    return jax.shard_map(
        body,
        mesh=mesh,
        in_specs=(
            P("dp", "mp"),
            P("dp", "mp", None),
            P(),
            P(None, None, "mp"),
            P("dp", None),
            P(),
            P("dp", "mp"),
        ),
        out_specs=(P("dp", "mp"), P("dp", "mp"), P(None, None, "mp"), P()),
        check_vma=False,
    )
```

```python
import functools

import jax
import jax.numpy as jnp
from jax import lax
from jax.experimental import pallas as pl
from jax.experimental.pallas import tpu as pltpu
from jax.sharding import PartitionSpec as P

HD = 128
BLOCK = 64
NEIGH = 2
NX, NY, NZ = 4, 4, 16
OWN = 4
UNITS = 8
REQ = 16
SLICE = 16
DE = 448
GAIN_PAD = 512
NMP = 8
PIECE = 32
NPIECE = DE // PIECE
QUARTERS = 4
ZPARTS = 2
QSLOTS = REQ // QUARTERS
F32 = jnp.float32
BF16 = jnp.bfloat16
MESH = pl.DeviceIdType.MESH


def dot(a, b, ca, cb):
    return lax.dot_general(a, b, (((ca,), (cb,)), ((), ())), preferred_element_type=F32)


def remote(src, dst, send, recv, to):
    return pltpu.make_async_remote_copy(
        src_ref=src, dst_ref=dst, send_sem=send, recv_sem=recv, device_id=to, device_id_type=MESH
    )


def kernel(
    states_hbm, gain_hbm, ids_hbm, place_hbm, w_hbm, q_hbm, g_hbm,
    out_hbm, dq_hbm, gkv_hbm, ggain_ref,
    states_ref, gain_ref, ids_ref, place_ref, w_ref, q_ref, g_ref, load_sem,
    out_ref, dq_ref, gkv_ref, store_sem,
    zbuf, idbuf, ids_s, out_x, from_x, nb,
    grad, xs, xr, acc, zs, rbuf, full, gm, gx, gz,
    id_send, id_recv, id_local, zr_send, zr_recv, zl_send, zl_recv,
    x_send, x_recv, y_send, y_recv, s_send, s_recv,
    rx_send, rx_recv, rz_send, rz_recv, gz_send, gz_recv, gx_send, gx_recv,
    m_send, m_recv, h_send, h_recv, v_send, v_recv,
):
    dp = lax.axis_index("dp")
    mp = lax.axis_index("mp")
    x, z, y, c = dp // NZ, dp % NZ, mp // 2, mp % 2
    to_z = lambda k: (x * NZ + (z + k + NZ) % NZ, mp)
    to_x = lambda k: ((x + k) % NX * NZ + z, mp)
    to_y = lambda k: (dp, (y + k) % NY * 2 + c)
    sib = (dp, y * 2 + 1 - c)
    sent = []

    def start(cp):
        cp.start()
        sent.append(cp)
        return cp

    loads = [
        pltpu.make_async_copy(src, dst, load_sem.at[i])
        for i, (src, dst) in enumerate(
            (
                (states_hbm, states_ref), (gain_hbm, gain_ref), (ids_hbm, ids_ref),
                (place_hbm, place_ref), (w_hbm, w_ref), (q_hbm, q_ref), (g_hbm, g_ref),
            )
        )
    ]
    for cp in loads:
        cp.start()

    barrier = pltpu.get_barrier_semaphore()
    near = [to_z(1), to_z(-1), to_z(2), to_z(-2), to_x(1), to_x(2), to_x(3), to_y(1), to_y(2), to_y(3), sib]
    for peer in near:
        pl.semaphore_signal(barrier, inc=1, device_id=peer, device_id_type=MESH)

    for cp in loads[:4]:
        cp.wait()
    own = states_ref[...].astype(F32)
    normed = own * lax.rsqrt(jnp.mean(own * own, -1, keepdims=True) + 1e-6)
    zbuf[pl.ds(z * OWN, OWN)] = (normed * gain_ref[...]).astype(BF16)
    lane = lax.broadcasted_iota(jnp.int32, (8, 128), 1)
    vec = jnp.zeros((8, 128), jnp.int32)
    for r in range(REQ):
        vec = jnp.where(lane == r, place_ref[ids_ref[r % NEIGH, r // NEIGH]], vec)
    idbuf[x] = vec

    pl.semaphore_wait(barrier, len(near))

    def z_copy(d, part, right):
        st = 2 - d % 2
        at = ((z - d + st + NZ) % NZ if right else (z + d - st) % NZ) * OWN + part * (OWN // ZPARTS)
        ref = zbuf.at[pl.ds(at, OWN // ZPARTS)]
        if right:
            return remote(ref, ref, zr_send.at[d - 1, part], zr_recv.at[d - 1, part], to_z(st))
        return remote(ref, ref, zl_send.at[d - 1, part], zl_recv.at[d - 1, part], to_z(-st))

    chains = [(right, part) for part in range(ZPARTS) for right in (True, False)]
    reach = {(right, part): 8 if right == (part % 2 == 0) else 7 for right, part in chains}
    live = {}
    for d in (2, 1):
        for right, part in chains:
            live[right, part, d] = start(z_copy(d, part, right))
    id_copies = [
        start(remote(idbuf.at[x], idbuf.at[x], id_send.at[k - 1], id_recv.at[k - 1], to_x(k)))
        for k in (2, 1, 3)
    ]
    for d in (2, 4, 6):
        for right, part in chains:
            live[right, part, d].wait_recv()
            for e in (d + 2, d + 1):
                if e <= reach[right, part]:
                    live[right, part, e] = start(z_copy(e, part, right))
        if d == 2:
            for cp in id_copies:
                cp.wait_recv()
            local = pltpu.make_async_copy(idbuf, ids_s, id_local)
            local.start()
            local.wait()
    for (right, part, d), cp in live.items():
        if d not in (2, 4, 6):
            cp.wait_recv()

    def wanted(who, r):
        p = ids_s[who, 0, r]
        return lax.rem(p, NZ * OWN), lax.div(p, NZ * OWN)

    x_copies = {}
    for j in range(QUARTERS):
        for k in (2, 1, 3):
            for r in range(j * QSLOTS, (j + 1) * QSLOTS):
                out_x[k - 1, r] = zbuf[wanted((x + k) % NX, r)[0]]
            slots = pl.ds(j * QSLOTS, QSLOTS)
            x_copies[k, j] = start(
                remote(
                    out_x.at[k - 1, slots], from_x.at[k - 1, slots],
                    x_send.at[k - 1, j], x_recv.at[k - 1, j], to_x(k),
                )
            )

    y_copies, s_copies = {}, {}

    def finish(j):
        for k in (1, 3, 2):
            x_copies[k, j].wait_recv()
        for r in range(j * QSLOTS, (j + 1) * QSLOTS):
            at, col = wanted(x, r)
            block = zbuf[at]
            for k in (1, 2, 3):
                block = jnp.where(col == (x + NX - k) % NX, from_x[k - 1, r], block)
            nb[mp, r] = block
        ref = nb.at[mp, pl.ds(j * QSLOTS, QSLOTS)]
        for k in (2, 1, 3):
            y_copies[k, j] = start(remote(ref, ref, y_send.at[k - 1, j], y_recv.at[k - 1, j], to_y(k)))
        s_copies[0, j] = start(remote(ref, ref, s_send.at[0, j], s_recv.at[0, j], sib))

    def relay(j):
        for k in (1, 3, 2):
            y_copies[k, j].wait_recv()
            ref = nb.at[(y + NY - k) % NY * 2 + c, pl.ds(j * QSLOTS, QSLOTS)]
            s_copies[k, j] = start(remote(ref, ref, s_send.at[k, j], s_recv.at[k, j], sib))

    scale = HD ** (-0.5)

    def attend(j):
        for k in range(4):
            s_copies[k, j].wait_recv()
        units = range(2 * j, 2 * j + 2)
        encs = [nb[:, NEIGH * u:NEIGH * (u + 1)].reshape(NMP * NEIGH * SLICE, DE) for u in units]
        keys = [dot(e, w_ref[0], 1, 0).astype(BF16) for e in encs]
        values = [dot(e, w_ref[1], 1, 0).astype(BF16) for e in encs]
        cells = []
        for i, u in enumerate(units):
            for h in range(2):
                rows, cols = slice(u * BLOCK, (u + 1) * BLOCK), slice(h * HD, (h + 1) * HD)
                cells.append((rows, cols, q_ref[rows, cols], g_ref[rows, cols], keys[i][:, cols], values[i][:, cols]))
        ss = [dot(q, k, 1, 1) * scale for _, _, q, g, k, v in cells]
        dps = [dot(g, v, 1, 1) for _, _, q, g, k, v in cells]
        es = [jnp.exp(s - jnp.max(s, -1, keepdims=True)) for s in ss]
        ps = [e / jnp.sum(e, -1, keepdims=True) for e in es]
        pbs = [p.astype(BF16) for p in ps]
        dss = [
            (p * (dp_ - jnp.sum(dp_ * p, -1, keepdims=True)) * scale).astype(BF16)
            for p, dp_ in zip(ps, dps)
        ]
        dks, dvs = [], []
        for (rows, cols, q, g, k, v), pb, ds in zip(cells, pbs, dss):
            out_ref[rows, cols] = dot(pb, v, 1, 0).astype(BF16)
            dq_ref[rows, cols] = dot(ds, k, 1, 0).astype(BF16)
            dks.append(dot(ds, q, 0, 0).astype(BF16))
            dvs.append(dot(pb, g, 0, 0).astype(BF16))
        enc = jnp.concatenate(encs, axis=0)
        dk = jnp.concatenate([jnp.concatenate(dks[0:2], axis=1), jnp.concatenate(dks[2:4], axis=1)], axis=0)
        dv = jnp.concatenate([jnp.concatenate(dvs[0:2], axis=1), jnp.concatenate(dvs[2:4], axis=1)], axis=0)
        for side, d in enumerate((dk, dv)):
            total = dot(enc, d, 0, 0)
            for h in range(2):
                part = total[:, h * HD:(h + 1) * HD]
                if j == 0:
                    grad[2 * side + h] = part
                else:
                    grad[2 * side + h] += part

    for step in range(QUARTERS + 2):
        if step < QUARTERS:
            finish(step)
        if 0 <= step - 1 < QUARTERS:
            relay(step - 1)
        if step == 2:
            for cp in loads[4:]:
                cp.wait()
        if 0 <= step - 2 < QUARTERS:
            attend(step - 2)

    stores = [
        pltpu.make_async_copy(out_ref, out_hbm, store_sem.at[0]),
        pltpu.make_async_copy(dq_ref, dq_hbm, store_sem.at[1]),
    ]
    for cp in stores:
        cp.start()

    HALF = DE // 2
    rx = {}
    for half in range(2):
        span = slice(half * HALF, (half + 1) * HALF)
        at = pl.ds(half * HALF, HALF)
        for k in (2, 1, 3):
            xs[k - 1, span] = grad[(x + k) % NX, span].astype(BF16)
            rx[k, half] = start(
                remote(xs.at[k - 1, at], xr.at[k - 1, at], rx_send.at[k - 1, half], rx_recv.at[k - 1, half], to_x(k))
            )

    prod = jnp.zeros((DE, HD), F32)
    for j in range(4):
        prod = prod + w_ref[j // 2, :, (j % 2) * HD:(j % 2 + 1) * HD].astype(F32) * grad[j]
    part = lax.dot_general(
        jnp.ones((8, HD), F32), prod, (((1,), (1,)), ((), ())),
        precision=lax.Precision.HIGHEST, preferred_element_type=F32,
    )[0:1] / gain_ref[...]
    gm[mp] = jnp.concatenate([part, jnp.zeros((1, GAIN_PAD - DE), F32)], axis=1)
    m_copies = [
        start(remote(gm.at[mp], gm.at[mp], m_send.at[k - 1], m_recv.at[k - 1], (dp, (mp + k) % NMP)))
        for k in range(1, NMP)
    ]

    def rows_of(t):
        return pl.ds(pl.multiple_of((t // 2 + NPIECE // 2 * (t % 2)) * PIECE, PIECE), PIECE)

    def z_out(t):
        return remote(zs.at[rows_of(t)], rbuf.at[z], rz_send.at[t], rz_recv.at[z], (x * NZ + t, mp))

    def sum_x(half):
        for k in (1, 3, 2):
            rx[k, half].wait_recv()
        span = slice(half * HALF, (half + 1) * HALF)
        total = grad[x, span]
        for k in (1, 2, 3):
            total = total + xr[k - 1, span].astype(F32)
        acc[span] = total
        zs[span] = total.astype(BF16)
        for t in range(half, NPIECE, 2):
            pl.when(z != t)(z_out(t).start)

    sum_x(0)
    for cp in m_copies:
        cp.wait_recv()
    gx[x] = functools.reduce(lambda s, m: s + gm[m], range(1, NMP), gm[0])
    h_copies = [
        start(remote(gx.at[x], gx.at[x], h_send.at[k - 1], h_recv.at[k - 1], to_x(k))) for k in (2, 1, 3)
    ]
    sum_x(1)
    for cp in h_copies:
        cp.wait_recv()
    gz[z] = functools.reduce(lambda s, m: s + gx[m], range(1, NX), gx[0])
    v_copies = [
        start(remote(gz.at[z], gz.at[z], v_send.at[k - 1], v_recv.at[k - 1], to_z(k)))
        for k in range(1, NZ)
    ]

    def z_back(k):
        ref = full.at[x, rows_of(z)]
        return remote(ref, ref, gz_send.at[k - 1], gz_recv.at[z], to_z(k))

    @pl.when(z < NPIECE)
    def _():
        rbuf[z] = jnp.zeros((PIECE, HD), BF16)
        for s in range(NZ):
            arrival = remote(zs.at[rows_of(0)], rbuf.at[s], rz_send.at[s], rz_recv.at[s], to_z(1))
            pl.when(z != s)(arrival.wait_recv)
        total = acc[rows_of(z)]
        for s in range(NZ):
            total = total + rbuf[s].astype(F32)
        full[x, rows_of(z)] = total.astype(BF16)
        for k in range(1, NZ):
            z_back(k).start()

    back = {}
    for half in range(2):
        for t in range(half, NPIECE, 2):
            ref = full.at[x, rows_of(t)]
            pl.when(z != t)(remote(ref, ref, gz_send.at[0], gz_recv.at[t], to_z(1)).wait_recv)
        ref = full.at[x, pl.ds(half * HALF, HALF)]
        for k in (2, 1, 3):
            back[k, half] = start(remote(ref, ref, gx_send.at[k - 1, half], gx_recv.at[k - 1, half], to_x(k)))

    for cp in v_copies:
        cp.wait_recv()
    g = functools.reduce(lambda s, m: s + gz[m], range(1, NZ), gz[0])
    ggain_ref[...] = g[:, :DE]

    for half in range(2):
        for k in (1, 3, 2):
            back[k, half].wait_recv()
        span = slice(half * HALF, (half + 1) * HALF)
        for j in range(4):
            gkv_ref[j // 2, span, (j % 2) * HD:(j % 2 + 1) * HD] = full[j, span]
        at = pl.ds(half * HALF, HALF)
        cp = pltpu.make_async_copy(gkv_ref.at[:, at], gkv_hbm.at[:, at], store_sem.at[2 + half])
        cp.start()
        stores.append(cp)

    for t in range(NPIECE):
        pl.when(z != t)(z_out(t).wait_send)

    @pl.when(z < NPIECE)
    def _():
        for k in range(1, NZ):
            z_back(k).wait_send()

    for cp in sent:
        cp.wait_send()
    for cp in stores:
        cp.wait()


def hand_over_kernel(*refs):
    n = (len(refs) - 1) // 3
    src, dst, held, sem = refs[:n], refs[n:2 * n], refs[2 * n:3 * n], refs[-1]
    first = [pltpu.make_async_copy(src[i], held[i], sem.at[i]) for i in range(n)]
    second = [pltpu.make_async_copy(held[i], dst[i], sem.at[n + i]) for i in range(n)]
    for cp in first:
        cp.start()
    for a, b in zip(first, second):
        a.wait()
        b.start()
    for cp in second:
        cp.wait()


def hand_over(results):
    n = len(results)
    hbm = pl.BlockSpec(memory_space=pltpu.HBM)
    return pl.pallas_call(
        hand_over_kernel,
        out_shape=tuple(jax.ShapeDtypeStruct(r.shape, r.dtype) for r in results),
        in_specs=[hbm] * n,
        out_specs=(hbm,) * n,
        scratch_shapes=[pltpu.VMEM(r.shape, r.dtype) for r in results] + [pltpu.SemaphoreType.DMA((2 * n,))],
        compiler_params=pltpu.CompilerParams(vmem_limit_bytes=56 * 1024 * 1024),
        name="hand_over",
    )(*results)


def body(queries, states, gain, w_kv, neighbour_ids, block_place, grad_out):
    dma = pltpu.SemaphoreType.DMA
    vmem = pltpu.VMEM
    block = (SLICE, DE)
    tok, cols = queries.shape
    hbm = pl.BlockSpec(memory_space=pltpu.HBM)
    out_spec = pl.BlockSpec(memory_space=pltpu.VMEM)
    results = pl.pallas_call(
        kernel,
        out_shape=(
            jax.ShapeDtypeStruct((tok, cols), BF16),
            jax.ShapeDtypeStruct((tok, cols), BF16),
            jax.ShapeDtypeStruct((2, DE, cols), BF16),
            jax.ShapeDtypeStruct((1, DE), F32),
        ),
        in_specs=[hbm] * 7,
        out_specs=(hbm,) * 3 + (out_spec,),
        scratch_shapes=[
            vmem(states.shape, BF16),
            vmem((1, DE), F32),
            pltpu.SMEM(neighbour_ids.shape[::-1], jnp.int32),
            pltpu.SMEM(block_place.shape, jnp.int32),
            vmem(w_kv.shape, BF16),
            vmem((tok, cols), BF16),
            vmem((tok, cols), BF16),
            dma((7,)),
            vmem((tok, cols), BF16),
            vmem((tok, cols), BF16),
            vmem(w_kv.shape, BF16),
            dma((4,)),
            vmem((NZ * OWN,) + block, BF16),
            vmem((NX, 8, 128), jnp.int32),
            pltpu.SMEM((NX, 8, 128), jnp.int32),
            vmem((3, REQ) + block, BF16),
            vmem((3, REQ) + block, BF16),
            vmem((NMP, REQ) + block, BF16),
            vmem((4, DE, HD), F32),
            vmem((3, DE, HD), BF16),
            vmem((3, DE, HD), BF16),
            vmem((DE, HD), F32),
            vmem((DE, HD), BF16),
            vmem((NZ, PIECE, HD), BF16),
            vmem((NX, DE, HD), BF16),
            vmem((NMP, 1, GAIN_PAD), F32),
            vmem((NX, 1, GAIN_PAD), F32),
            vmem((NZ, 1, GAIN_PAD), F32),
            dma((3,)), dma((3,)), dma,
            dma((8, ZPARTS)), dma((8, ZPARTS)), dma((8, ZPARTS)), dma((8, ZPARTS)),
            dma((3, QUARTERS)), dma((3, QUARTERS)),
            dma((3, QUARTERS)), dma((3, QUARTERS)),
            dma((4, QUARTERS)), dma((4, QUARTERS)),
            dma((3, 2)), dma((3, 2)), dma((NZ,)), dma((NZ,)), dma((NZ,)), dma((NZ,)),
            dma((3, 2)), dma((3, 2)),
            dma((NMP,)), dma((NMP,)), dma((3,)), dma((3,)), dma((NZ,)), dma((NZ,)),
        ],
        compiler_params=pltpu.CompilerParams(
            collective_id=0, has_side_effects=True, vmem_limit_bytes=56 * 1024 * 1024
        ),
        name="retro_step",
    )(states, gain.reshape(1, DE), neighbour_ids.T, block_place, w_kv, queries, grad_out)
    attended, d_query, grad_kv, grad_gain = hand_over(results)
    return attended, d_query, grad_kv, grad_gain.reshape(DE)


def solution(mesh):
    return jax.shard_map(
        body,
        mesh=mesh,
        in_specs=(
            P("dp", "mp"),
            P("dp", "mp", None),
            P(),
            P(None, None, "mp"),
            P("dp", None),
            P(),
            P("dp", "mp"),
        ),
        out_specs=(P("dp", "mp"), P("dp", "mp"), P(None, None, "mp"), P()),
        check_vma=False,
    )
```

```python
import functools

import jax
import jax.numpy as jnp
from jax import lax
from jax.experimental import pallas as pl
from jax.experimental.pallas import tpu as pltpu
from jax.sharding import PartitionSpec as P

HD = 128
BLOCK = 64
NEIGH = 2
NX, NY, NZ = 4, 4, 16
OWN = 4
UNITS = 8
REQ = 16
SLICE = 16
DE = 448
GAIN_PAD = 512
NMP = 8
PIECE = 32
NPIECE = DE // PIECE
PAIRS = REQ // 2
TILES = 7
WINDOW = 2
LAG = 3
GROUPS = {7: ((0, 1, 2, 3),), 10: ((4, 5, 6, 7),)}
LANES = 128
F32 = jnp.float32
BF16 = jnp.bfloat16
MESH = pl.DeviceIdType.MESH


def dot(a, b, ca, cb):
    return lax.dot_general(a, b, (((ca,), (cb,)), ((), ())), preferred_element_type=F32)


def remote(src, dst, send, recv, to):
    return pltpu.make_async_remote_copy(
        src_ref=src, dst_ref=dst, send_sem=send, recv_sem=recv, device_id=to, device_id_type=MESH
    )


def kernel(
    states_hbm, gain_hbm, ids_hbm, place_hbm, w_hbm, q_hbm, g_hbm,
    out_hbm, dq_hbm, gkv_hbm, ggain_ref,
    states_ref, gain_ref, ids_ref, place_ref, w_ref, q_ref, g_ref, load_sem,
    out_ref, dq_ref, gkv_ref, store_sem,
    zbuf, idbuf, ids_s, out_x, from_x, nb,
    grad, xs, xr, acc, zs, rbuf, gm, gx, gz,
    id_send, id_recv, id_local, zr_send, zr_recv, zl_send, zl_recv,
    x_send, x_recv, y_send, y_recv, s_send, s_recv,
    rx_send, rx_recv, rz_send, rz_recv, gz_send, gz_recv, gx_send, gx_recv,
    m_send, m_recv, h_send, h_recv, v_send, v_recv,
):
    dp = lax.axis_index("dp")
    mp = lax.axis_index("mp")
    x, z, y, c = dp // NZ, dp % NZ, mp // 2, mp % 2
    to_z = lambda k: (x * NZ + (z + k + NZ) % NZ, mp)
    to_x = lambda k: ((x + k) % NX * NZ + z, mp)
    to_y = lambda k: (dp, (y + k) % NY * 2 + c)
    sib = (dp, y * 2 + 1 - c)
    sent = []

    def start(cp):
        cp.start()
        sent.append(cp)
        return cp

    loads = [
        pltpu.make_async_copy(src, dst, load_sem.at[i])
        for i, (src, dst) in enumerate(
            (
                (states_hbm, states_ref), (gain_hbm, gain_ref), (ids_hbm, ids_ref),
                (place_hbm, place_ref), (w_hbm, w_ref), (q_hbm, q_ref), (g_hbm, g_ref),
            )
        )
    ]
    for cp in loads:
        cp.start()

    barrier = pltpu.get_barrier_semaphore()
    near = [to_z(1), to_z(-1), to_z(2), to_z(-2), to_x(1), to_x(2), to_x(3), to_y(1), to_y(2), to_y(3), sib]
    for peer in near:
        pl.semaphore_signal(barrier, inc=1, device_id=peer, device_id_type=MESH)

    for cp in loads[:4]:
        cp.wait()
    own = states_ref[...].astype(F32)
    normed = own * lax.rsqrt(jnp.mean(own * own, -1, keepdims=True) + 1e-6)
    encoded = normed * gain_ref[...]
    for i in range(OWN // 2):
        a, b = encoded[2 * i], encoded[2 * i + 1]
        tiles = [t[:, j * LANES:(j + 1) * LANES] for t in (a, b) for j in range(3)]
        tiles.append(jnp.concatenate([a[:, 3 * LANES:], b[:, 3 * LANES:]], axis=1))
        for j, tile in enumerate(tiles):
            zbuf[z * (OWN // 2) + i, j] = tile.astype(BF16)
    pl.semaphore_wait(barrier, len(near))

    ZPARTS = OWN // 2

    def z_copy(d, part, right):
        st = 2 - d % 2
        at = ((z - d + st + NZ) % NZ if right else (z + d - st) % NZ) * ZPARTS + part
        ref = zbuf.at[at]
        if right:
            return remote(ref, ref, zr_send.at[d - 1, part], zr_recv.at[d - 1, part], to_z(st))
        return remote(ref, ref, zl_send.at[d - 1, part], zl_recv.at[d - 1, part], to_z(-st))

    chains = [(right, part) for part in range(ZPARTS) for right in (True, False)]
    reach = {(right, part): 8 if right == (part % 2 == 0) else 7 for right, part in chains}
    live = {}
    def z_start(d):
        for right, part in chains:
            if d <= reach[right, part]:
                live[right, part, d] = start(z_copy(d, part, right))

    z_start(2)
    z_start(1)

    lane = lax.broadcasted_iota(jnp.int32, (8, LANES), 1)
    vec = jnp.zeros((8, LANES), jnp.int32)
    for r in range(REQ):
        vec = jnp.where(lane == r, place_ref[ids_ref[r % NEIGH, r // NEIGH]], vec)
    idbuf[x] = vec
    id_copies = [
        start(remote(idbuf.at[x], idbuf.at[x], id_send.at[k - 1], id_recv.at[k - 1], to_x(k)))
        for k in (2, 1, 3)
    ]
    for d in (2, 4, 6):
        for right, part in chains:
            live[right, part, d].wait_recv()
            if d + 2 <= reach[right, part]:
                live[right, part, d + 2] = start(z_copy(d + 2, part, right))
        z_start(d + 1)
        if d == 2:
            for cp in id_copies:
                cp.wait_recv()
            local = pltpu.make_async_copy(idbuf, ids_s, id_local)
            local.start()
            local.wait()
    for (right, part, d), cp in live.items():
        if d not in (2, 4, 6):
            cp.wait_recv()

    low_half = lax.broadcasted_iota(jnp.int32, (SLICE, LANES), 1) < LANES // 2

    def wanted(who, r):
        p = ids_s[who, 0, r]
        return lax.rem(p, NZ * OWN), lax.div(p, NZ * OWN)

    def pick_pair(who, i):
        tiles, tails = [], []
        for n in range(2):
            at = wanted(who, 2 * i + n)[0]
            pair, odd = lax.div(at, 2), lax.rem(at, 2)
            tiles += [zbuf[pair, 3 * odd + j] for j in range(3)]
            tail = zbuf[pair, 6].astype(F32)
            tails.append(jnp.where(odd == n, tail, pltpu.roll(tail, LANES // 2, 1)))
        tiles.append(jnp.where(low_half, tails[0], tails[1]).astype(BF16))
        return tiles

    x_copies = {}

    def ask(i):
        for k in (2, 1, 3):
            for j, tile in enumerate(pick_pair((x + k) % NX, i)):
                out_x[k - 1, i, j] = tile
            if i >= WINDOW:
                x_copies[k, i - WINDOW].wait_send()
            x_copies[k, i] = remote(
                out_x.at[k - 1, i], from_x.at[k - 1, i], x_send.at[k - 1, i], x_recv.at[k - 1, i], to_x(k)
            )
            x_copies[k, i].start()

    y_copies, s_copies = {}, {}

    def finish(i):
        for k in (1, 3, 2):
            x_copies[k, i].wait_recv()
        cols = [wanted(x, 2 * i + n)[1] for n in range(2)]
        for j, tile in enumerate(pick_pair(x, i)):
            for k in (1, 2, 3):
                at = (x + NX - k) % NX
                if j < 6:
                    here = cols[j // 3] == at
                else:
                    here = jnp.where(low_half, cols[0], cols[1]) == at
                tile = jnp.where(here, from_x[k - 1, i, j].astype(F32), tile.astype(F32)).astype(BF16)
            nb[mp, i, j] = tile
        ref = nb.at[mp, i]
        for k in (2, 1, 3):
            y_copies[k, i] = start(remote(ref, ref, y_send.at[k - 1, i], y_recv.at[k - 1, i], to_y(k)))
        s_copies[0, i] = start(remote(ref, ref, s_send.at[0, i], s_recv.at[0, i], sib))

    def relay(i):
        for k in (1, 3, 2):
            y_copies[k, i].wait_recv()
            ref = nb.at[(y + NY - k) % NY * 2 + c, i]
            s_copies[k, i] = start(remote(ref, ref, s_send.at[k, i], s_recv.at[k, i], sib))

    def rows_of_unit(u):
        rows = NMP * SLICE
        main = [nb[:, u, j].reshape(rows, LANES) for j in range(6)]
        tail = nb[:, u, 6].reshape(rows, LANES).astype(F32)
        second = pltpu.roll(tail, LANES // 2, 1)
        ends = [t[:, :LANES // 2].astype(BF16) for t in (tail, second)]
        return jnp.concatenate(
            [jnp.concatenate(main[3 * n:3 * n + 3] + [ends[n]], axis=1) for n in range(2)], axis=0
        )

    scale = HD ** (-0.5)

    def attend(units):
        for u in units:
            for k in range(4):
                s_copies[k, u].wait_recv()
        encs = [rows_of_unit(u) for u in units]
        keys = [dot(e, w_ref[0], 1, 0).astype(BF16) for e in encs]
        values = [dot(e, w_ref[1], 1, 0).astype(BF16) for e in encs]
        cells = []
        for i, u in enumerate(units):
            for h in range(2):
                rows, cols = slice(u * BLOCK, (u + 1) * BLOCK), slice(h * HD, (h + 1) * HD)
                cells.append((rows, cols, q_ref[rows, cols], g_ref[rows, cols], keys[i][:, cols], values[i][:, cols]))
        ss = [dot(q, k, 1, 1) * scale for _, _, q, g, k, v in cells]
        dps = [dot(g, v, 1, 1) for _, _, q, g, k, v in cells]
        es = [jnp.exp(s - jnp.max(s, -1, keepdims=True)) for s in ss]
        ps = [e / jnp.sum(e, -1, keepdims=True) for e in es]
        pbs = [p.astype(BF16) for p in ps]
        dss = [
            (p * (dp_ - jnp.sum(dp_ * p, -1, keepdims=True)) * scale).astype(BF16)
            for p, dp_ in zip(ps, dps)
        ]
        dks, dvs = [], []
        for (rows, cols, q, g, k, v), pb, ds in zip(cells, pbs, dss):
            out_ref[rows, cols] = dot(pb, v, 1, 0).astype(BF16)
            dq_ref[rows, cols] = dot(ds, k, 1, 0).astype(BF16)
            dks.append(dot(ds, q, 0, 0).astype(BF16))
            dvs.append(dot(pb, g, 0, 0).astype(BF16))
        enc = jnp.concatenate(encs, axis=0)
        dk, dv = (
            jnp.concatenate(
                [jnp.concatenate(d[2 * n:2 * n + 2], axis=1) for n in range(len(units))], axis=0
            )
            for d in (dks, dvs)
        )
        for side, d in enumerate((dk, dv)):
            total = dot(enc, d, 0, 0)
            for h in range(2):
                part = total[:, h * HD:(h + 1) * HD]
                if units[0] == 0:
                    grad[2 * side + h] = part
                else:
                    grad[2 * side + h] += part

    for i in range(PAIRS + LAG + 3):
        if i < PAIRS:
            ask(i)
        if 0 <= i - LAG < PAIRS:
            finish(i - LAG)
        if 0 <= i - LAG - 3 < PAIRS:
            relay(i - LAG - 3)
        if i == LAG + 4:
            for cp in loads[4:]:
                cp.wait()
        for units in GROUPS.get(i - LAG, ()):
            attend(units)
    for k in (1, 2, 3):
        for i in range(PAIRS - WINDOW, PAIRS):
            x_copies[k, i].wait_send()

    stores = [
        pltpu.make_async_copy(out_ref, out_hbm, store_sem.at[0]),
        pltpu.make_async_copy(dq_ref, dq_hbm, store_sem.at[1]),
    ]
    for cp in stores:
        cp.start()

    rx = {}
    for i in range(NPIECE // 2):
        span = slice(2 * i * PIECE, (2 * i + 2) * PIECE)
        at = pl.ds(2 * i * PIECE, 2 * PIECE)
        for k in (2, 1, 3):
            xs[k - 1, span] = grad[(x + k) % NX, span].astype(BF16)
            rx[k, i] = start(
                remote(xs.at[k - 1, at], xr.at[k - 1, at], rx_send.at[k - 1, i], rx_recv.at[k - 1, i], to_x(k))
            )

    prod = jnp.zeros((DE, HD), F32)
    for j in range(4):
        prod = prod + w_ref[j // 2, :, (j % 2) * HD:(j % 2 + 1) * HD].astype(F32) * grad[j]
    part = lax.dot_general(
        jnp.ones((8, HD), F32), prod, (((1,), (1,)), ((), ())),
        precision=lax.Precision.HIGHEST, preferred_element_type=F32,
    )[0:1] / gain_ref[...]
    gm[mp] = jnp.concatenate([part, jnp.zeros((1, GAIN_PAD - DE), F32)], axis=1)
    m_copies = [
        start(remote(gm.at[mp], gm.at[mp], m_send.at[k - 1], m_recv.at[k - 1], (dp, (mp + k) % NMP)))
        for k in range(1, NMP)
    ]

    def rows_of(t):
        return pl.ds(pl.multiple_of((t // 2 + NPIECE // 2 * (t % 2)) * PIECE, PIECE), PIECE)

    def z_out(t):
        return remote(zs.at[rows_of(t)], rbuf.at[z], rz_send.at[t], rz_recv.at[z], (x * NZ + t, mp))

    def sum_x(i):
        for k in (1, 3, 2):
            rx[k, i].wait_recv()
        span = slice(2 * i * PIECE, (2 * i + 2) * PIECE)
        total = grad[x, span]
        for k in (1, 2, 3):
            total = total + xr[k - 1, span].astype(F32)
        acc[span] = total
        zs[span] = total.astype(BF16)
        for p in (2 * i, 2 * i + 1):
            t = 2 * p if p < NPIECE // 2 else 2 * p + 1 - NPIECE
            pl.when(z != t)(z_out(t).start)

    for i in range(NPIECE // 2):
        sum_x(i)
        if i == 2:
            for cp in m_copies:
                cp.wait_recv()
            gx[x] = functools.reduce(lambda s, m: s + gm[m], range(1, NMP), gm[0])
            h_copies = [
                start(remote(gx.at[x], gx.at[x], h_send.at[k - 1], h_recv.at[k - 1], to_x(k)))
                for k in (2, 1, 3)
            ]
    for cp in h_copies:
        cp.wait_recv()
    gz[z] = functools.reduce(lambda s, m: s + gx[m], range(1, NX), gx[0])
    by_distance = sorted(range(1, NZ), key=lambda k: -min(k, NZ - k))
    v_copies = [
        start(remote(gz.at[z], gz.at[z], v_send.at[k - 1], v_recv.at[k - 1], to_z(k))) for k in by_distance
    ]

    def part_of(j, rows):
        return gkv_ref.at[j // 2, rows, pl.ds(pl.multiple_of(j % 2 * HD, HD), HD)]

    def z_back(k):
        ref = part_of(x, rows_of(z))
        return remote(ref, ref, gz_send.at[k - 1], gz_recv.at[z], to_z(k))

    @pl.when(z < NPIECE)
    def _():
        rbuf[z] = jnp.zeros((PIECE, HD), BF16)
        for s in range(NZ):
            arrival = remote(zs.at[rows_of(0)], rbuf.at[s], rz_send.at[s], rz_recv.at[s], to_z(1))
            pl.when(z != s)(arrival.wait_recv)
        total = acc[rows_of(z)]
        for s in range(NZ):
            total = total + rbuf[s].astype(F32)
        part_of(x, rows_of(z))[...] = total.astype(BF16)
        for k in by_distance:
            z_back(k).start()

    HALF = DE // 2
    back = {}
    for half in range(2):
        for t in range(half, NPIECE, 2):
            ref = part_of(x, rows_of(t))
            pl.when(z != t)(remote(ref, ref, gz_send.at[0], gz_recv.at[t], to_z(1)).wait_recv)
        ref = part_of(x, pl.ds(half * HALF, HALF))
        for k in (2, 1, 3):
            back[k, half] = start(remote(ref, ref, gx_send.at[k - 1, half], gx_recv.at[k - 1, half], to_x(k)))

    for cp in v_copies:
        cp.wait_recv()
    g = functools.reduce(lambda s, m: s + gz[m], range(1, NZ), gz[0])
    ggain_ref[...] = g[:, :DE]

    for half in range(2):
        for k in (1, 3, 2):
            back[k, half].wait_recv()
        at = pl.ds(half * HALF, HALF)
        cp = pltpu.make_async_copy(gkv_ref.at[:, at], gkv_hbm.at[:, at], store_sem.at[2 + half])
        cp.start()
        stores.append(cp)

    for t in range(NPIECE):
        pl.when(z != t)(z_out(t).wait_send)

    @pl.when(z < NPIECE)
    def _():
        for k in range(1, NZ):
            z_back(k).wait_send()

    for cp in sent:
        cp.wait_send()
    for cp in stores:
        cp.wait()


def hand_over_kernel(*refs):
    n = (len(refs) - 1) // 3
    src, dst, held, sem = refs[:n], refs[n:2 * n], refs[2 * n:3 * n], refs[-1]
    first = [pltpu.make_async_copy(src[i], held[i], sem.at[i]) for i in range(n)]
    second = [pltpu.make_async_copy(held[i], dst[i], sem.at[n + i]) for i in range(n)]
    for cp in first:
        cp.start()
    for a, b in zip(first, second):
        a.wait()
        b.start()
    for cp in second:
        cp.wait()


def hand_over(results):
    n = len(results)
    hbm = pl.BlockSpec(memory_space=pltpu.HBM)
    return pl.pallas_call(
        hand_over_kernel,
        out_shape=tuple(jax.ShapeDtypeStruct(r.shape, r.dtype) for r in results),
        in_specs=[hbm] * n,
        out_specs=(hbm,) * n,
        scratch_shapes=[pltpu.VMEM(r.shape, r.dtype) for r in results] + [pltpu.SemaphoreType.DMA((2 * n,))],
        compiler_params=pltpu.CompilerParams(vmem_limit_bytes=56 * 1024 * 1024),
        name="hand_over",
    )(*results)


def body(queries, states, gain, w_kv, neighbour_ids, block_place, grad_out):
    dma = pltpu.SemaphoreType.DMA
    vmem = pltpu.VMEM
    pair = (TILES, SLICE, LANES)
    tok, cols = queries.shape
    hbm = pl.BlockSpec(memory_space=pltpu.HBM)
    out_spec = pl.BlockSpec(memory_space=pltpu.VMEM)
    results = pl.pallas_call(
        kernel,
        out_shape=(
            jax.ShapeDtypeStruct((tok, cols), BF16),
            jax.ShapeDtypeStruct((tok, cols), BF16),
            jax.ShapeDtypeStruct((2, DE, cols), BF16),
            jax.ShapeDtypeStruct((1, DE), F32),
        ),
        in_specs=[hbm] * 7,
        out_specs=(hbm,) * 3 + (out_spec,),
        scratch_shapes=[
            vmem(states.shape, BF16),
            vmem((1, DE), F32),
            pltpu.SMEM(neighbour_ids.shape[::-1], jnp.int32),
            pltpu.SMEM(block_place.shape, jnp.int32),
            vmem(w_kv.shape, BF16),
            vmem((tok, cols), BF16),
            vmem((tok, cols), BF16),
            dma((7,)),
            vmem((tok, cols), BF16),
            vmem((tok, cols), BF16),
            vmem(w_kv.shape, BF16),
            dma((4,)),
            vmem((NZ * OWN // 2,) + pair, BF16),
            vmem((NX, 8, 128), jnp.int32),
            pltpu.SMEM((NX, 8, 128), jnp.int32),
            vmem((3, PAIRS) + pair, BF16),
            vmem((3, PAIRS) + pair, BF16),
            vmem((NMP, PAIRS) + pair, BF16),
            vmem((4, DE, HD), F32),
            vmem((3, DE, HD), BF16),
            vmem((3, DE, HD), BF16),
            vmem((DE, HD), F32),
            vmem((DE, HD), BF16),
            vmem((NZ, PIECE, HD), BF16),
            vmem((NMP, 1, GAIN_PAD), F32),
            vmem((NX, 1, GAIN_PAD), F32),
            vmem((NZ, 1, GAIN_PAD), F32),
            dma((3,)), dma((3,)), dma,
            dma((8, 2)), dma((8, 2)), dma((8, 2)), dma((8, 2)),
            dma((3, PAIRS)), dma((3, PAIRS)),
            dma((3, PAIRS)), dma((3, PAIRS)),
            dma((4, PAIRS)), dma((4, PAIRS)),
            dma((3, NPIECE)), dma((3, NPIECE)), dma((NZ,)), dma((NZ,)), dma((NZ,)), dma((NZ,)),
            dma((3, 2)), dma((3, 2)),
            dma((NMP,)), dma((NMP,)), dma((3,)), dma((3,)), dma((NZ,)), dma((NZ,)),
        ],
        compiler_params=pltpu.CompilerParams(
            collective_id=0, has_side_effects=True, vmem_limit_bytes=56 * 1024 * 1024
        ),
        name="retro_step",
    )(states, gain.reshape(1, DE), neighbour_ids.T, block_place, w_kv, queries, grad_out)
    attended, d_query, grad_kv, grad_gain = hand_over(results)
    return attended, d_query, grad_kv, grad_gain.reshape(DE)


def solution(mesh):
    return jax.shard_map(
        body,
        mesh=mesh,
        in_specs=(
            P("dp", "mp"),
            P("dp", "mp", None),
            P(),
            P(None, None, "mp"),
            P("dp", None),
            P(),
            P("dp", "mp"),
        ),
        out_specs=(P("dp", "mp"), P("dp", "mp"), P(None, None, "mp"), P()),
        check_vma=False,
    )
```

```python
import functools

import jax
import jax.numpy as jnp
from jax import lax
from jax.experimental import pallas as pl
from jax.experimental.pallas import tpu as pltpu
from jax.sharding import PartitionSpec as P

HD = 128
BLOCK = 64
NEIGH = 2
NX, NY, NZ = 4, 4, 16
OWN = 4
UNITS = 8
REQ = 16
SLICE = 16
DE = 448
GAIN_PAD = 512
NMP = 8
PIECE = 32
NPIECE = DE // PIECE
PAIRS = REQ // 2
TILES = 7
ODD_AFTER = {0: (), 2: (1,), 4: (3, 5), 6: (7,)}
WINDOW = 3
LAG = 4
GROUPS = {7: ((0, 1, 2, 3),), 10: ((4, 5, 6, 7),)}
LANES = 128
F32 = jnp.float32
BF16 = jnp.bfloat16
MESH = pl.DeviceIdType.MESH


def dot(a, b, ca, cb):
    return lax.dot_general(a, b, (((ca,), (cb,)), ((), ())), preferred_element_type=F32)


def remote(src, dst, send, recv, to):
    return pltpu.make_async_remote_copy(
        src_ref=src, dst_ref=dst, send_sem=send, recv_sem=recv, device_id=to, device_id_type=MESH
    )


def kernel(
    states_hbm, gain_hbm, ids_hbm, place_hbm, w_hbm, q_hbm, g_hbm,
    out_hbm, dq_hbm, gkv_hbm, ggain_ref,
    states_ref, gain_ref, ids_ref, place_ref, w_ref, q_ref, g_ref, load_sem,
    out_ref, dq_ref, gkv_ref, store_sem,
    zbuf, idbuf, ids_s, out_x, from_x, nb,
    grad, xs, xr, acc, zs, rbuf, full, gm, gx, gz,
    id_send, id_recv, id_local, zr_send, zr_recv, zl_send, zl_recv,
    x_send, x_recv, y_send, y_recv, s_send, s_recv,
    rx_send, rx_recv, rz_send, rz_recv, gz_send, gz_recv, gx_send, gx_recv,
    m_send, m_recv, h_send, h_recv, v_send, v_recv,
):
    dp = lax.axis_index("dp")
    mp = lax.axis_index("mp")
    x, z, y, c = dp // NZ, dp % NZ, mp // 2, mp % 2
    to_z = lambda k: (x * NZ + (z + k + NZ) % NZ, mp)
    to_x = lambda k: ((x + k) % NX * NZ + z, mp)
    to_y = lambda k: (dp, (y + k) % NY * 2 + c)
    sib = (dp, y * 2 + 1 - c)
    sent = []

    def start(cp):
        cp.start()
        sent.append(cp)
        return cp

    loads = [
        pltpu.make_async_copy(src, dst, load_sem.at[i])
        for i, (src, dst) in enumerate(
            (
                (states_hbm, states_ref), (gain_hbm, gain_ref), (ids_hbm, ids_ref),
                (place_hbm, place_ref), (w_hbm, w_ref), (q_hbm, q_ref), (g_hbm, g_ref),
            )
        )
    ]
    for cp in loads:
        cp.start()

    barrier = pltpu.get_barrier_semaphore()
    near = [to_z(1), to_z(-1), to_z(2), to_z(-2), to_x(1), to_x(2), to_x(3), to_y(1), to_y(2), to_y(3), sib]
    for peer in near:
        pl.semaphore_signal(barrier, inc=1, device_id=peer, device_id_type=MESH)

    for cp in loads[:4]:
        cp.wait()
    own = states_ref[...].astype(F32)
    normed = own * lax.rsqrt(jnp.mean(own * own, -1, keepdims=True) + 1e-6)
    encoded = normed * gain_ref[...]
    for i in range(OWN // 2):
        a, b = encoded[2 * i], encoded[2 * i + 1]
        tiles = [t[:, j * LANES:(j + 1) * LANES] for t in (a, b) for j in range(3)]
        tiles.append(jnp.concatenate([a[:, 3 * LANES:], b[:, 3 * LANES:]], axis=1))
        for j, tile in enumerate(tiles):
            zbuf[z * (OWN // 2) + i, j] = tile.astype(BF16)
    pl.semaphore_wait(barrier, len(near))

    ZPARTS = OWN // 2

    def z_copy(d, part, right):
        st = 2 - d % 2
        at = ((z - d + st + NZ) % NZ if right else (z + d - st) % NZ) * ZPARTS + part
        ref = zbuf.at[at]
        if right:
            return remote(ref, ref, zr_send.at[d - 1, part], zr_recv.at[d - 1, part], to_z(st))
        return remote(ref, ref, zl_send.at[d - 1, part], zl_recv.at[d - 1, part], to_z(-st))

    chains = [(right, part) for part in range(ZPARTS) for right in (True, False)]
    reach = {(right, part): 8 if right == (part % 2 == 0) else 7 for right, part in chains}
    live = {}
    def z_start(d):
        for right, part in chains:
            if d <= reach[right, part]:
                live[right, part, d] = start(z_copy(d, part, right))

    z_start(2)
    for d in ODD_AFTER[0]:
        z_start(d)

    lane = lax.broadcasted_iota(jnp.int32, (8, LANES), 1)
    vec = jnp.zeros((8, LANES), jnp.int32)
    for r in range(REQ):
        vec = jnp.where(lane == r, place_ref[ids_ref[r % NEIGH, r // NEIGH]], vec)
    idbuf[x] = vec
    id_copies = [
        start(remote(idbuf.at[x], idbuf.at[x], id_send.at[k - 1], id_recv.at[k - 1], to_x(k)))
        for k in (2, 1, 3)
    ]
    for d in (2, 4, 6):
        for right, part in chains:
            live[right, part, d].wait_recv()
            if d + 2 <= reach[right, part]:
                live[right, part, d + 2] = start(z_copy(d + 2, part, right))
        for e in ODD_AFTER[d]:
            z_start(e)
        if d == 2:
            for cp in id_copies:
                cp.wait_recv()
            local = pltpu.make_async_copy(idbuf, ids_s, id_local)
            local.start()
            local.wait()
    for (right, part, d), cp in live.items():
        if d not in (2, 4, 6):
            cp.wait_recv()

    low_half = lax.broadcasted_iota(jnp.int32, (SLICE, LANES), 1) < LANES // 2

    def wanted(who, r):
        p = ids_s[who, 0, r]
        return lax.rem(p, NZ * OWN), lax.div(p, NZ * OWN)

    def pick_pair(who, i):
        tiles, tails = [], []
        for n in range(2):
            at = wanted(who, 2 * i + n)[0]
            pair, odd = lax.div(at, 2), lax.rem(at, 2)
            tiles += [zbuf[pair, 3 * odd + j] for j in range(3)]
            tail = zbuf[pair, 6].astype(F32)
            tails.append(jnp.where(odd == n, tail, pltpu.roll(tail, LANES // 2, 1)))
        tiles.append(jnp.where(low_half, tails[0], tails[1]).astype(BF16))
        return tiles

    x_copies = {}

    def ask(i):
        for k in (2, 1, 3):
            for j, tile in enumerate(pick_pair((x + k) % NX, i)):
                out_x[k - 1, i, j] = tile
            if i >= WINDOW:
                x_copies[k, i - WINDOW].wait_send()
            x_copies[k, i] = remote(
                out_x.at[k - 1, i], from_x.at[k - 1, i], x_send.at[k - 1, i], x_recv.at[k - 1, i], to_x(k)
            )
            x_copies[k, i].start()

    y_copies, s_copies = {}, {}

    def finish(i):
        for k in (1, 3, 2):
            x_copies[k, i].wait_recv()
        cols = [wanted(x, 2 * i + n)[1] for n in range(2)]
        for j, tile in enumerate(pick_pair(x, i)):
            for k in (1, 2, 3):
                at = (x + NX - k) % NX
                if j < 6:
                    here = cols[j // 3] == at
                else:
                    here = jnp.where(low_half, cols[0], cols[1]) == at
                tile = jnp.where(here, from_x[k - 1, i, j].astype(F32), tile.astype(F32)).astype(BF16)
            nb[mp, i, j] = tile
        ref = nb.at[mp, i]
        for k in (2, 1, 3):
            y_copies[k, i] = start(remote(ref, ref, y_send.at[k - 1, i], y_recv.at[k - 1, i], to_y(k)))
        s_copies[0, i] = start(remote(ref, ref, s_send.at[0, i], s_recv.at[0, i], sib))

    def relay(i):
        for k in (1, 3, 2):
            y_copies[k, i].wait_recv()
            ref = nb.at[(y + NY - k) % NY * 2 + c, i]
            s_copies[k, i] = start(remote(ref, ref, s_send.at[k, i], s_recv.at[k, i], sib))

    def rows_of_unit(u):
        rows = NMP * SLICE
        main = [nb[:, u, j].reshape(rows, LANES) for j in range(6)]
        tail = nb[:, u, 6].reshape(rows, LANES).astype(F32)
        second = pltpu.roll(tail, LANES // 2, 1)
        ends = [t[:, :LANES // 2].astype(BF16) for t in (tail, second)]
        return jnp.concatenate(
            [jnp.concatenate(main[3 * n:3 * n + 3] + [ends[n]], axis=1) for n in range(2)], axis=0
        )

    scale = HD ** (-0.5)

    def attend(units):
        for u in units:
            for k in range(4):
                s_copies[k, u].wait_recv()
        encs = [rows_of_unit(u) for u in units]
        keys = [dot(e, w_ref[0], 1, 0).astype(BF16) for e in encs]
        values = [dot(e, w_ref[1], 1, 0).astype(BF16) for e in encs]
        cells = []
        for i, u in enumerate(units):
            for h in range(2):
                rows, cols = slice(u * BLOCK, (u + 1) * BLOCK), slice(h * HD, (h + 1) * HD)
                cells.append((rows, cols, q_ref[rows, cols], g_ref[rows, cols], keys[i][:, cols], values[i][:, cols]))
        ss = [dot(q, k, 1, 1) * scale for _, _, q, g, k, v in cells]
        dps = [dot(g, v, 1, 1) for _, _, q, g, k, v in cells]
        es = [jnp.exp(s - jnp.max(s, -1, keepdims=True)) for s in ss]
        ps = [e / jnp.sum(e, -1, keepdims=True) for e in es]
        pbs = [p.astype(BF16) for p in ps]
        dss = [
            (p * (dp_ - jnp.sum(dp_ * p, -1, keepdims=True)) * scale).astype(BF16)
            for p, dp_ in zip(ps, dps)
        ]
        dks, dvs = [], []
        for (rows, cols, q, g, k, v), pb, ds in zip(cells, pbs, dss):
            out_ref[rows, cols] = dot(pb, v, 1, 0).astype(BF16)
            dq_ref[rows, cols] = dot(ds, k, 1, 0).astype(BF16)
            dks.append(dot(ds, q, 0, 0).astype(BF16))
            dvs.append(dot(pb, g, 0, 0).astype(BF16))
        enc = jnp.concatenate(encs, axis=0)
        dk, dv = (
            jnp.concatenate(
                [jnp.concatenate(d[2 * n:2 * n + 2], axis=1) for n in range(len(units))], axis=0
            )
            for d in (dks, dvs)
        )
        for side, d in enumerate((dk, dv)):
            total = dot(enc, d, 0, 0)
            for h in range(2):
                part = total[:, h * HD:(h + 1) * HD]
                if units[0] == 0:
                    grad[2 * side + h] = part
                else:
                    grad[2 * side + h] += part

    for i in range(PAIRS + LAG + 3):
        if i < PAIRS:
            ask(i)
        if 0 <= i - LAG < PAIRS:
            finish(i - LAG)
        if 0 <= i - LAG - 3 < PAIRS:
            relay(i - LAG - 3)
        if i == LAG + 4:
            for cp in loads[4:]:
                cp.wait()
        for units in GROUPS.get(i - LAG, ()):
            attend(units)
    for k in (1, 2, 3):
        for i in range(PAIRS - WINDOW, PAIRS):
            x_copies[k, i].wait_send()

    stores = [
        pltpu.make_async_copy(out_ref, out_hbm, store_sem.at[0]),
        pltpu.make_async_copy(dq_ref, dq_hbm, store_sem.at[1]),
    ]
    for cp in stores:
        cp.start()

    def rows_of(t):
        return pl.ds(pl.multiple_of((t // 2 + NPIECE // 2 * (t % 2)) * PIECE, PIECE), PIECE)

    by_distance = sorted(range(1, NZ), key=lambda k: -min(k, NZ - k))

    def x_out(k, t):
        src, dst = xs.at[k - 1, rows_of(t)], xr.at[k - 1, rows_of(t)]
        return remote(src, dst, rx_send.at[k - 1, t], rx_recv.at[k - 1, t], to_x(k))

    for d in by_distance + [0]:
        t = (z + d) % NZ

        @pl.when(t < NPIECE)
        def _():
            for k in (2, 1, 3):
                xs[k - 1, rows_of(t)] = grad[(x + k) % NX, rows_of(t)].astype(BF16)
                x_out(k, t).start()

    prod = jnp.zeros((DE, HD), F32)
    for j in range(4):
        prod = prod + w_ref[j // 2, :, (j % 2) * HD:(j % 2 + 1) * HD].astype(F32) * grad[j]
    part = lax.dot_general(
        jnp.ones((8, HD), F32), prod, (((1,), (1,)), ((), ())),
        precision=lax.Precision.HIGHEST, preferred_element_type=F32,
    )[0:1] / gain_ref[...]
    gm[mp] = jnp.concatenate([part, jnp.zeros((1, GAIN_PAD - DE), F32)], axis=1)
    m_copies = [
        start(remote(gm.at[mp], gm.at[mp], m_send.at[k - 1], m_recv.at[k - 1], (dp, (mp + k) % NMP)))
        for k in range(1, NMP)
    ]

    def z_out(t):
        return remote(zs.at[rows_of(t)], rbuf.at[z], rz_send.at[t], rz_recv.at[z], (x * NZ + t, mp))

    for n, d in enumerate(by_distance + [0]):
        t = (z + d) % NZ

        @pl.when(t < NPIECE)
        def _():
            for k in (1, 3, 2):
                x_out(k, t).wait_recv()
            total = grad[x, rows_of(t)]
            for k in (1, 2, 3):
                total = total + xr[k - 1, rows_of(t)].astype(F32)
            if d == 0:
                acc[...] = total
            else:
                zs[rows_of(t)] = total.astype(BF16)
                z_out(t).start()

        if n == 7:
            for cp in m_copies:
                cp.wait_recv()
            gx[x] = functools.reduce(lambda s, m: s + gm[m], range(1, NMP), gm[0])
            h_copies = [
                start(remote(gx.at[x], gx.at[x], h_send.at[k - 1], h_recv.at[k - 1], to_x(k)))
                for k in (2, 1, 3)
            ]
    for cp in h_copies:
        cp.wait_recv()
    gz[z] = functools.reduce(lambda s, m: s + gx[m], range(1, NX), gx[0])
    v_copies = [
        start(remote(gz.at[z], gz.at[z], v_send.at[k - 1], v_recv.at[k - 1], to_z(k))) for k in by_distance
    ]

    def part_of(j, rows):
        return full.at[j, rows]

    def z_back(k):
        ref = part_of(x, rows_of(z))
        return remote(ref, ref, gz_send.at[k - 1], gz_recv.at[z], to_z(k))

    @pl.when(z < NPIECE)
    def _():
        rbuf[z] = jnp.zeros((PIECE, HD), BF16)
        for s in range(NZ):
            arrival = remote(zs.at[rows_of(0)], rbuf.at[s], rz_send.at[s], rz_recv.at[s], to_z(1))
            pl.when(z != s)(arrival.wait_recv)
        total = acc[...]
        for s in range(NZ):
            total = total + rbuf[s].astype(F32)
        part_of(x, rows_of(z))[...] = total.astype(BF16)
        for k in by_distance:
            z_back(k).start()

    HALF = DE // 2
    back = {}
    for half in range(2):
        for t in range(half, NPIECE, 2):
            ref = part_of(x, rows_of(t))
            pl.when(z != t)(remote(ref, ref, gz_send.at[0], gz_recv.at[t], to_z(1)).wait_recv)
        ref = part_of(x, pl.ds(half * HALF, HALF))
        for k in (2, 1, 3):
            back[k, half] = start(remote(ref, ref, gx_send.at[k - 1, half], gx_recv.at[k - 1, half], to_x(k)))

    for cp in v_copies:
        cp.wait_recv()
    g = functools.reduce(lambda s, m: s + gz[m], range(1, NZ), gz[0])
    ggain_ref[...] = g[:, :DE]

    for half in range(2):
        for k in (1, 3, 2):
            back[k, half].wait_recv()
        span = slice(half * HALF, (half + 1) * HALF)
        for j in range(4):
            gkv_ref[j // 2, span, (j % 2) * HD:(j % 2 + 1) * HD] = full[j, span]
        at = pl.ds(half * HALF, HALF)
        cp = pltpu.make_async_copy(gkv_ref.at[:, at], gkv_hbm.at[:, at], store_sem.at[2 + half])
        cp.start()
        stores.append(cp)

    for t in range(NPIECE):
        pl.when(z != t)(z_out(t).wait_send)
        for k in (1, 2, 3):
            x_out(k, t).wait_send()

    @pl.when(z < NPIECE)
    def _():
        for k in range(1, NZ):
            z_back(k).wait_send()

    for cp in sent:
        cp.wait_send()
    for cp in stores:
        cp.wait()


def hand_over_kernel(*refs):
    n = (len(refs) - 1) // 3
    src, dst, held, sem = refs[:n], refs[n:2 * n], refs[2 * n:3 * n], refs[-1]
    first = [pltpu.make_async_copy(src[i], held[i], sem.at[i]) for i in range(n)]
    second = [pltpu.make_async_copy(held[i], dst[i], sem.at[n + i]) for i in range(n)]
    for cp in first:
        cp.start()
    for a, b in zip(first, second):
        a.wait()
        b.start()
    for cp in second:
        cp.wait()


def hand_over(results):
    n = len(results)
    hbm = pl.BlockSpec(memory_space=pltpu.HBM)
    return pl.pallas_call(
        hand_over_kernel,
        out_shape=tuple(jax.ShapeDtypeStruct(r.shape, r.dtype) for r in results),
        in_specs=[hbm] * n,
        out_specs=(hbm,) * n,
        scratch_shapes=[pltpu.VMEM(r.shape, r.dtype) for r in results] + [pltpu.SemaphoreType.DMA((2 * n,))],
        compiler_params=pltpu.CompilerParams(vmem_limit_bytes=56 * 1024 * 1024),
        name="hand_over",
    )(*results)


def body(queries, states, gain, w_kv, neighbour_ids, block_place, grad_out):
    dma = pltpu.SemaphoreType.DMA
    vmem = pltpu.VMEM
    pair = (TILES, SLICE, LANES)
    tok, cols = queries.shape
    hbm = pl.BlockSpec(memory_space=pltpu.HBM)
    out_spec = pl.BlockSpec(memory_space=pltpu.VMEM)
    results = pl.pallas_call(
        kernel,
        out_shape=(
            jax.ShapeDtypeStruct((tok, cols), BF16),
            jax.ShapeDtypeStruct((tok, cols), BF16),
            jax.ShapeDtypeStruct((2, DE, cols), BF16),
            jax.ShapeDtypeStruct((1, DE), F32),
        ),
        in_specs=[hbm] * 7,
        out_specs=(hbm,) * 3 + (out_spec,),
        scratch_shapes=[
            vmem(states.shape, BF16),
            vmem((1, DE), F32),
            pltpu.SMEM(neighbour_ids.shape[::-1], jnp.int32),
            pltpu.SMEM(block_place.shape, jnp.int32),
            vmem(w_kv.shape, BF16),
            vmem((tok, cols), BF16),
            vmem((tok, cols), BF16),
            dma((7,)),
            vmem((tok, cols), BF16),
            vmem((tok, cols), BF16),
            vmem(w_kv.shape, BF16),
            dma((4,)),
            vmem((NZ * OWN // 2,) + pair, BF16),
            vmem((NX, 8, 128), jnp.int32),
            pltpu.SMEM((NX, 8, 128), jnp.int32),
            vmem((3, PAIRS) + pair, BF16),
            vmem((3, PAIRS) + pair, BF16),
            vmem((NMP, PAIRS) + pair, BF16),
            vmem((4, DE, HD), F32),
            vmem((3, DE, HD), BF16),
            vmem((3, DE, HD), BF16),
            vmem((PIECE, HD), F32),
            vmem((DE, HD), BF16),
            vmem((NZ, PIECE, HD), BF16),
            vmem((NX, DE, HD), BF16),
            vmem((NMP, 1, GAIN_PAD), F32),
            vmem((NX, 1, GAIN_PAD), F32),
            vmem((NZ, 1, GAIN_PAD), F32),
            dma((3,)), dma((3,)), dma,
            dma((8, 2)), dma((8, 2)), dma((8, 2)), dma((8, 2)),
            dma((3, PAIRS)), dma((3, PAIRS)),
            dma((3, PAIRS)), dma((3, PAIRS)),
            dma((4, PAIRS)), dma((4, PAIRS)),
            dma((3, NPIECE)), dma((3, NPIECE)), dma((NZ,)), dma((NZ,)), dma((NZ,)), dma((NZ,)),
            dma((3, 2)), dma((3, 2)),
            dma((NMP,)), dma((NMP,)), dma((3,)), dma((3,)), dma((NZ,)), dma((NZ,)),
        ],
        compiler_params=pltpu.CompilerParams(
            collective_id=0, has_side_effects=True, vmem_limit_bytes=56 * 1024 * 1024
        ),
        name="retro_step",
    )(states, gain.reshape(1, DE), neighbour_ids.T, block_place, w_kv, queries, grad_out)
    attended, d_query, grad_kv, grad_gain = hand_over(results)
    return attended, d_query, grad_kv, grad_gain.reshape(DE)


def solution(mesh):
    return jax.shard_map(
        body,
        mesh=mesh,
        in_specs=(
            P("dp", "mp"),
            P("dp", "mp", None),
            P(),
            P(None, None, "mp"),
            P("dp", None),
            P(),
            P("dp", "mp"),
        ),
        out_specs=(P("dp", "mp"), P("dp", "mp"), P(None, None, "mp"), P()),
        check_vma=False,
    )
```

```python
import functools

import jax
import jax.numpy as jnp
from jax import lax
from jax.experimental import pallas as pl
from jax.experimental.pallas import tpu as pltpu
from jax.sharding import PartitionSpec as P

HD = 128
BLOCK = 64
NEIGH = 2
NX, NY, NZ = 4, 4, 16
OWN = 4
UNITS = 8
REQ = 16
SLICE = 16
DE = 448
GAIN_PAD = 512
NMP = 8
PIECE = 32
NPIECE = DE // PIECE
PAIRS = REQ // 2
TILES = 7
ODD_AFTER = {0: (), 2: (1,), 4: (3, 5), 6: (7,)}
WINDOW = 4
LAG = 4
GROUPS = {7: ((0, 1, 2, 3),), 10: ((4, 5, 6, 7),)}
LANES = 128
F32 = jnp.float32
BF16 = jnp.bfloat16
MESH = pl.DeviceIdType.MESH


def dot(a, b, ca, cb):
    return lax.dot_general(a, b, (((ca,), (cb,)), ((), ())), preferred_element_type=F32)


def remote(src, dst, send, recv, to):
    return pltpu.make_async_remote_copy(
        src_ref=src, dst_ref=dst, send_sem=send, recv_sem=recv, device_id=to, device_id_type=MESH
    )


def kernel(
    states_hbm, gain_hbm, ids_hbm, place_hbm, w_hbm, q_hbm, g_hbm,
    out_hbm, dq_hbm, gkv_hbm, ggain_ref,
    states_ref, gain_ref, ids_ref, place_ref, w_ref, q_ref, g_ref, load_sem,
    out_ref, dq_ref, gkv_ref, store_sem,
    zbuf, idbuf, ids_s, out_x, from_x, nb,
    grad, xs, xr, acc, zs, rbuf, full, gm, gx, gz,
    id_send, id_recv, id_local, zr_send, zr_recv, zl_send, zl_recv,
    x_send, x_recv, y_send, y_recv, s_send, s_recv,
    rx_send, rx_recv, rz_send, rz_recv, gz_send, gz_recv, gx_send, gx_recv,
    m_send, m_recv, h_send, h_recv, v_send, v_recv,
):
    dp = lax.axis_index("dp")
    mp = lax.axis_index("mp")
    x, z, y, c = dp // NZ, dp % NZ, mp // 2, mp % 2
    to_z = lambda k: (x * NZ + (z + k + NZ) % NZ, mp)
    to_x = lambda k: ((x + k) % NX * NZ + z, mp)
    to_y = lambda k: (dp, (y + k) % NY * 2 + c)
    sib = (dp, y * 2 + 1 - c)
    sent = []

    def start(cp):
        cp.start()
        sent.append(cp)
        return cp

    loads = [
        pltpu.make_async_copy(src, dst, load_sem.at[i])
        for i, (src, dst) in enumerate(
            (
                (states_hbm, states_ref), (gain_hbm, gain_ref), (ids_hbm, ids_ref),
                (place_hbm, place_ref), (w_hbm, w_ref), (q_hbm, q_ref), (g_hbm, g_ref),
            )
        )
    ]
    for cp in loads:
        cp.start()

    barrier = pltpu.get_barrier_semaphore()
    near = [to_z(1), to_z(-1), to_z(2), to_z(-2), to_x(1), to_x(2), to_x(3), to_y(1), to_y(2), to_y(3), sib]
    for peer in near:
        pl.semaphore_signal(barrier, inc=1, device_id=peer, device_id_type=MESH)

    for cp in loads[:4]:
        cp.wait()
    own = states_ref[...].astype(F32)
    normed = own * lax.rsqrt(jnp.mean(own * own, -1, keepdims=True) + 1e-6)
    encoded = normed * gain_ref[...]
    for i in range(OWN // 2):
        a, b = encoded[2 * i], encoded[2 * i + 1]
        tiles = [t[:, j * LANES:(j + 1) * LANES] for t in (a, b) for j in range(3)]
        tiles.append(jnp.concatenate([a[:, 3 * LANES:], b[:, 3 * LANES:]], axis=1))
        for j, tile in enumerate(tiles):
            zbuf[z * (OWN // 2) + i, j] = tile.astype(BF16)
    pl.semaphore_wait(barrier, len(near))

    ZPARTS = OWN // 2

    def z_copy(d, part, right):
        st = 2 - d % 2
        at = ((z - d + st + NZ) % NZ if right else (z + d - st) % NZ) * ZPARTS + part
        ref = zbuf.at[at]
        if right:
            return remote(ref, ref, zr_send.at[d - 1, part], zr_recv.at[d - 1, part], to_z(st))
        return remote(ref, ref, zl_send.at[d - 1, part], zl_recv.at[d - 1, part], to_z(-st))

    chains = [(right, part) for part in range(ZPARTS) for right in (True, False)]
    reach = {(right, part): 8 if right == (part % 2 == 0) else 7 for right, part in chains}
    live = {}
    def z_start(d):
        for right, part in chains:
            if d <= reach[right, part]:
                live[right, part, d] = start(z_copy(d, part, right))

    z_start(2)
    for d in ODD_AFTER[0]:
        z_start(d)

    lane = lax.broadcasted_iota(jnp.int32, (8, LANES), 1)
    vec = jnp.zeros((8, LANES), jnp.int32)
    for r in range(REQ):
        vec = jnp.where(lane == r, place_ref[ids_ref[r % NEIGH, r // NEIGH]], vec)
    idbuf[x] = vec
    id_copies = [
        start(remote(idbuf.at[x], idbuf.at[x], id_send.at[k - 1], id_recv.at[k - 1], to_x(k)))
        for k in (2, 1, 3)
    ]
    for d in (2, 4, 6):
        for right, part in chains:
            live[right, part, d].wait_recv()
            if d + 2 <= reach[right, part]:
                live[right, part, d + 2] = start(z_copy(d + 2, part, right))
        for e in ODD_AFTER[d]:
            z_start(e)
        if d == 2:
            for cp in id_copies:
                cp.wait_recv()
            local = pltpu.make_async_copy(idbuf, ids_s, id_local)
            local.start()
            local.wait()
    for (right, part, d), cp in live.items():
        if d not in (2, 4, 6):
            cp.wait_recv()

    low_half = lax.broadcasted_iota(jnp.int32, (SLICE, LANES), 1) < LANES // 2

    def wanted(who, r):
        p = ids_s[who, 0, r]
        return lax.rem(p, NZ * OWN), lax.div(p, NZ * OWN)

    def pick_pair(who, i):
        tiles, tails = [], []
        for n in range(2):
            at = wanted(who, 2 * i + n)[0]
            pair, odd = lax.div(at, 2), lax.rem(at, 2)
            tiles += [zbuf[pair, 3 * odd + j] for j in range(3)]
            tail = zbuf[pair, 6].astype(F32)
            tails.append(jnp.where(odd == n, tail, pltpu.roll(tail, LANES // 2, 1)))
        tiles.append(jnp.where(low_half, tails[0], tails[1]).astype(BF16))
        return tiles

    x_copies = {}

    def ask(i):
        for k in ((2, 1, 3) if i % 2 == 0 else (3, 1, 2)):
            for j, tile in enumerate(pick_pair((x + k) % NX, i)):
                out_x[k - 1, i, j] = tile
            if i >= WINDOW:
                x_copies[k, i - WINDOW].wait_send()
            x_copies[k, i] = remote(
                out_x.at[k - 1, i], from_x.at[k - 1, i], x_send.at[k - 1, i], x_recv.at[k - 1, i], to_x(k)
            )
            x_copies[k, i].start()

    y_copies, s_copies = {}, {}

    def finish(i):
        for k in (1, 3, 2):
            x_copies[k, i].wait_recv()
        cols = [wanted(x, 2 * i + n)[1] for n in range(2)]
        for j, tile in enumerate(pick_pair(x, i)):
            for k in (1, 2, 3):
                at = (x + NX - k) % NX
                if j < 6:
                    here = cols[j // 3] == at
                else:
                    here = jnp.where(low_half, cols[0], cols[1]) == at
                tile = jnp.where(here, from_x[k - 1, i, j].astype(F32), tile.astype(F32)).astype(BF16)
            nb[mp, i, j] = tile
        ref = nb.at[mp, i]
        for k in (2, 1, 3):
            y_copies[k, i] = start(remote(ref, ref, y_send.at[k - 1, i], y_recv.at[k - 1, i], to_y(k)))
        s_copies[0, i] = start(remote(ref, ref, s_send.at[0, i], s_recv.at[0, i], sib))

    def relay(i):
        for k in (1, 3, 2):
            y_copies[k, i].wait_recv()
            ref = nb.at[(y + NY - k) % NY * 2 + c, i]
            s_copies[k, i] = start(remote(ref, ref, s_send.at[k, i], s_recv.at[k, i], sib))

    def rows_of_unit(u):
        rows = NMP * SLICE
        main = [nb[:, u, j].reshape(rows, LANES) for j in range(6)]
        tail = nb[:, u, 6].reshape(rows, LANES).astype(F32)
        second = pltpu.roll(tail, LANES // 2, 1)
        ends = [t[:, :LANES // 2].astype(BF16) for t in (tail, second)]
        return jnp.concatenate(
            [jnp.concatenate(main[3 * n:3 * n + 3] + [ends[n]], axis=1) for n in range(2)], axis=0
        )

    scale = HD ** (-0.5)

    def attend(units):
        for u in units:
            for k in range(4):
                s_copies[k, u].wait_recv()
        encs = [rows_of_unit(u) for u in units]
        keys = [dot(e, w_ref[0], 1, 0).astype(BF16) for e in encs]
        values = [dot(e, w_ref[1], 1, 0).astype(BF16) for e in encs]
        cells = []
        for i, u in enumerate(units):
            for h in range(2):
                rows, cols = slice(u * BLOCK, (u + 1) * BLOCK), slice(h * HD, (h + 1) * HD)
                cells.append((rows, cols, q_ref[rows, cols], g_ref[rows, cols], keys[i][:, cols], values[i][:, cols]))
        ss = [dot(q, k, 1, 1) * scale for _, _, q, g, k, v in cells]
        dps = [dot(g, v, 1, 1) for _, _, q, g, k, v in cells]
        es = [jnp.exp(s - jnp.max(s, -1, keepdims=True)) for s in ss]
        ps = [e / jnp.sum(e, -1, keepdims=True) for e in es]
        pbs = [p.astype(BF16) for p in ps]
        dss = [
            (p * (dp_ - jnp.sum(dp_ * p, -1, keepdims=True)) * scale).astype(BF16)
            for p, dp_ in zip(ps, dps)
        ]
        dks, dvs = [], []
        for (rows, cols, q, g, k, v), pb, ds in zip(cells, pbs, dss):
            out_ref[rows, cols] = dot(pb, v, 1, 0).astype(BF16)
            dq_ref[rows, cols] = dot(ds, k, 1, 0).astype(BF16)
            dks.append(dot(ds, q, 0, 0).astype(BF16))
            dvs.append(dot(pb, g, 0, 0).astype(BF16))
        enc = jnp.concatenate(encs, axis=0)
        dk, dv = (
            jnp.concatenate(
                [jnp.concatenate(d[2 * n:2 * n + 2], axis=1) for n in range(len(units))], axis=0
            )
            for d in (dks, dvs)
        )
        for side, d in enumerate((dk, dv)):
            total = dot(enc, d, 0, 0)
            for h in range(2):
                part = total[:, h * HD:(h + 1) * HD]
                if units[0] == 0:
                    grad[2 * side + h] = part
                else:
                    grad[2 * side + h] += part

    for i in range(PAIRS + LAG + 3):
        if i < PAIRS:
            ask(i)
        if 0 <= i - LAG < PAIRS:
            finish(i - LAG)
        if 0 <= i - LAG - 3 < PAIRS:
            relay(i - LAG - 3)
        if i == LAG + 4:
            for cp in loads[4:]:
                cp.wait()
        for units in GROUPS.get(i - LAG, ()):
            attend(units)
    for k in (1, 2, 3):
        for i in range(PAIRS - WINDOW, PAIRS):
            x_copies[k, i].wait_send()

    stores = [
        pltpu.make_async_copy(out_ref, out_hbm, store_sem.at[0]),
        pltpu.make_async_copy(dq_ref, dq_hbm, store_sem.at[1]),
    ]
    for cp in stores:
        cp.start()

    def rows_of(t):
        return pl.ds(pl.multiple_of((t // 2 + NPIECE // 2 * (t % 2)) * PIECE, PIECE), PIECE)

    by_distance = sorted(range(1, NZ), key=lambda k: -min(k, NZ - k))

    def x_out(k, t):
        src, dst = xs.at[k - 1, rows_of(t)], xr.at[k - 1, rows_of(t)]
        return remote(src, dst, rx_send.at[k - 1, t], rx_recv.at[k - 1, t], to_x(k))

    for d in by_distance + [0]:
        t = (z + d) % NZ

        @pl.when(t < NPIECE)
        def _():
            for k in (2, 1, 3):
                xs[k - 1, rows_of(t)] = grad[(x + k) % NX, rows_of(t)].astype(BF16)
                x_out(k, t).start()

    prod = jnp.zeros((DE, HD), F32)
    for j in range(4):
        prod = prod + w_ref[j // 2, :, (j % 2) * HD:(j % 2 + 1) * HD].astype(F32) * grad[j]
    part = lax.dot_general(
        jnp.ones((8, HD), F32), prod, (((1,), (1,)), ((), ())),
        precision=lax.Precision.HIGHEST, preferred_element_type=F32,
    )[0:1] / gain_ref[...]
    gm[mp] = jnp.concatenate([part, jnp.zeros((1, GAIN_PAD - DE), F32)], axis=1)
    m_copies = [
        start(remote(gm.at[mp], gm.at[mp], m_send.at[k - 1], m_recv.at[k - 1], (dp, (mp + k) % NMP)))
        for k in range(1, NMP)
    ]

    def z_out(t):
        return remote(zs.at[rows_of(t)], rbuf.at[z], rz_send.at[t], rz_recv.at[z], (x * NZ + t, mp))

    for n, d in enumerate(by_distance + [0]):
        t = (z + d) % NZ

        @pl.when(t < NPIECE)
        def _():
            for k in (1, 3, 2):
                x_out(k, t).wait_recv()
            total = grad[x, rows_of(t)]
            for k in (1, 2, 3):
                total = total + xr[k - 1, rows_of(t)].astype(F32)
            if d == 0:
                acc[...] = total
            else:
                zs[rows_of(t)] = total.astype(BF16)
                z_out(t).start()

        if n == 7:
            for cp in m_copies:
                cp.wait_recv()
            gx[x] = functools.reduce(lambda s, m: s + gm[m], range(1, NMP), gm[0])
            h_copies = [
                start(remote(gx.at[x], gx.at[x], h_send.at[k - 1], h_recv.at[k - 1], to_x(k)))
                for k in (2, 1, 3)
            ]
    for cp in h_copies:
        cp.wait_recv()
    gz[z] = functools.reduce(lambda s, m: s + gx[m], range(1, NX), gx[0])
    v_copies = [
        start(remote(gz.at[z], gz.at[z], v_send.at[k - 1], v_recv.at[k - 1], to_z(k))) for k in by_distance
    ]

    def part_of(j, rows):
        return full.at[j, rows]

    def z_back(k):
        ref = part_of(x, rows_of(z))
        return remote(ref, ref, gz_send.at[k - 1], gz_recv.at[z], to_z(k))

    @pl.when(z < NPIECE)
    def _():
        rbuf[z] = jnp.zeros((PIECE, HD), BF16)
        for s in range(NZ):
            arrival = remote(zs.at[rows_of(0)], rbuf.at[s], rz_send.at[s], rz_recv.at[s], to_z(1))
            pl.when(z != s)(arrival.wait_recv)
        total = acc[...]
        for s in range(NZ):
            total = total + rbuf[s].astype(F32)
        part_of(x, rows_of(z))[...] = total.astype(BF16)
        for k in by_distance:
            z_back(k).start()

    HALF = DE // 2
    back = {}
    for half in range(2):
        for t in range(half, NPIECE, 2):
            ref = part_of(x, rows_of(t))
            pl.when(z != t)(remote(ref, ref, gz_send.at[0], gz_recv.at[t], to_z(1)).wait_recv)
        ref = part_of(x, pl.ds(half * HALF, HALF))
        for k in (2, 1, 3):
            back[k, half] = start(remote(ref, ref, gx_send.at[k - 1, half], gx_recv.at[k - 1, half], to_x(k)))

    for cp in v_copies:
        cp.wait_recv()
    g = functools.reduce(lambda s, m: s + gz[m], range(1, NZ), gz[0])
    ggain_ref[...] = g[:, :DE]

    for half in range(2):
        for k in (1, 3, 2):
            back[k, half].wait_recv()
        span = slice(half * HALF, (half + 1) * HALF)
        for j in range(4):
            gkv_ref[j // 2, span, (j % 2) * HD:(j % 2 + 1) * HD] = full[j, span]
        at = pl.ds(half * HALF, HALF)
        cp = pltpu.make_async_copy(gkv_ref.at[:, at], gkv_hbm.at[:, at], store_sem.at[2 + half])
        cp.start()
        stores.append(cp)

    for t in range(NPIECE):
        pl.when(z != t)(z_out(t).wait_send)
        for k in (1, 2, 3):
            x_out(k, t).wait_send()

    @pl.when(z < NPIECE)
    def _():
        for k in range(1, NZ):
            z_back(k).wait_send()

    for cp in sent:
        cp.wait_send()
    for cp in stores:
        cp.wait()


def hand_over_kernel(*refs):
    n = (len(refs) - 1) // 3
    src, dst, held, sem = refs[:n], refs[n:2 * n], refs[2 * n:3 * n], refs[-1]
    first = [pltpu.make_async_copy(src[i], held[i], sem.at[i]) for i in range(n)]
    second = [pltpu.make_async_copy(held[i], dst[i], sem.at[n + i]) for i in range(n)]
    for cp in first:
        cp.start()
    for a, b in zip(first, second):
        a.wait()
        b.start()
    for cp in second:
        cp.wait()


def hand_over(results):
    n = len(results)
    hbm = pl.BlockSpec(memory_space=pltpu.HBM)
    return pl.pallas_call(
        hand_over_kernel,
        out_shape=tuple(jax.ShapeDtypeStruct(r.shape, r.dtype) for r in results),
        in_specs=[hbm] * n,
        out_specs=(hbm,) * n,
        scratch_shapes=[pltpu.VMEM(r.shape, r.dtype) for r in results] + [pltpu.SemaphoreType.DMA((2 * n,))],
        compiler_params=pltpu.CompilerParams(vmem_limit_bytes=56 * 1024 * 1024),
        name="hand_over",
    )(*results)


def body(queries, states, gain, w_kv, neighbour_ids, block_place, grad_out):
    dma = pltpu.SemaphoreType.DMA
    vmem = pltpu.VMEM
    pair = (TILES, SLICE, LANES)
    tok, cols = queries.shape
    hbm = pl.BlockSpec(memory_space=pltpu.HBM)
    out_spec = pl.BlockSpec(memory_space=pltpu.VMEM)
    results = pl.pallas_call(
        kernel,
        out_shape=(
            jax.ShapeDtypeStruct((tok, cols), BF16),
            jax.ShapeDtypeStruct((tok, cols), BF16),
            jax.ShapeDtypeStruct((2, DE, cols), BF16),
            jax.ShapeDtypeStruct((1, DE), F32),
        ),
        in_specs=[hbm] * 7,
        out_specs=(hbm,) * 3 + (out_spec,),
        scratch_shapes=[
            vmem(states.shape, BF16),
            vmem((1, DE), F32),
            pltpu.SMEM(neighbour_ids.shape[::-1], jnp.int32),
            pltpu.SMEM(block_place.shape, jnp.int32),
            vmem(w_kv.shape, BF16),
            vmem((tok, cols), BF16),
            vmem((tok, cols), BF16),
            dma((7,)),
            vmem((tok, cols), BF16),
            vmem((tok, cols), BF16),
            vmem(w_kv.shape, BF16),
            dma((4,)),
            vmem((NZ * OWN // 2,) + pair, BF16),
            vmem((NX, 8, 128), jnp.int32),
            pltpu.SMEM((NX, 8, 128), jnp.int32),
            vmem((3, PAIRS) + pair, BF16),
            vmem((3, PAIRS) + pair, BF16),
            vmem((NMP, PAIRS) + pair, BF16),
            vmem((4, DE, HD), F32),
            vmem((3, DE, HD), BF16),
            vmem((3, DE, HD), BF16),
            vmem((PIECE, HD), F32),
            vmem((DE, HD), BF16),
            vmem((NZ, PIECE, HD), BF16),
            vmem((NX, DE, HD), BF16),
            vmem((NMP, 1, GAIN_PAD), F32),
            vmem((NX, 1, GAIN_PAD), F32),
            vmem((NZ, 1, GAIN_PAD), F32),
            dma((3,)), dma((3,)), dma,
            dma((8, 2)), dma((8, 2)), dma((8, 2)), dma((8, 2)),
            dma((3, PAIRS)), dma((3, PAIRS)),
            dma((3, PAIRS)), dma((3, PAIRS)),
            dma((4, PAIRS)), dma((4, PAIRS)),
            dma((3, NPIECE)), dma((3, NPIECE)), dma((NZ,)), dma((NZ,)), dma((NZ,)), dma((NZ,)),
            dma((3, 2)), dma((3, 2)),
            dma((NMP,)), dma((NMP,)), dma((3,)), dma((3,)), dma((NZ,)), dma((NZ,)),
        ],
        compiler_params=pltpu.CompilerParams(
            collective_id=0, has_side_effects=True, vmem_limit_bytes=56 * 1024 * 1024
        ),
        name="retro_step",
    )(states, gain.reshape(1, DE), neighbour_ids.T, block_place, w_kv, queries, grad_out)
    attended, d_query, grad_kv, grad_gain = hand_over(results)
    return attended, d_query, grad_kv, grad_gain.reshape(DE)


def solution(mesh):
    return jax.shard_map(
        body,
        mesh=mesh,
        in_specs=(
            P("dp", "mp"),
            P("dp", "mp", None),
            P(),
            P(None, None, "mp"),
            P("dp", None),
            P(),
            P("dp", "mp"),
        ),
        out_specs=(P("dp", "mp"), P("dp", "mp"), P(None, None, "mp"), P()),
        check_vma=False,
    )
```
